512 devices in a mesh: wide: 64 (over z_lo, y, core), narrow: 8 (over x, z_hi).
Axes of the slice: x: 4, y: 8, z: 8 (z_hi: 2, z_lo: 4; z = z_hi * 4 + z_lo), core: 2. Of those that a mesh axis runs over, the one named last changes fastest.
Arguments:
- features: bfloat16 [16, 1024, 2, 1024], P(None, 'wide', None, 'narrow'), may hold values from -6 to 6
- cotangent: bfloat16 [16, 1024, 2, 1024], P(None, 'wide', None, 'narrow'), may hold values from -6 to 6
- coarse_weight: bfloat16 [32, 16, 3, 3, 3], replicated, may hold values from -0.3125 to 0.3125
- fine_weight: bfloat16 [16, 48, 3, 3, 3], replicated, may hold values from -0.15625 to 0.15625
Outputs:
- output: bfloat16 [16, 1024, 2, 1024], P(None, 'wide', None, 'narrow')
- grad_features: bfloat16 [16, 1024, 2, 1024], P(None, 'wide', None, 'narrow')
- grad_fine: float32 [16, 48, 3, 3, 3], replicated
- grad_coarse: float32 [32, 16, 3, 3, 3], replicated
The draws below stay inside these ranges and needn't reach their ends.
All inputs are finite; a program needn't handle non-finite values.
Results may differ from the reference program's by a relative error of at most 0.012.
Values may be sent and summed in bfloat16 or wider, within the bound.
A program may use at most 64 MiB of HBM per device.

```python
import math
import jax
import jax.numpy as jnp
from jax import lax

C1 = 16
C2 = 32
PLANES = 2
NX = 1024
NY = 1024
CELLS = 2097152


def shard_levels(stream_key, dims, cuts, least, largest):
    level = 1.0
    for position, blocks in cuts:
        heights = jax.random.uniform(jax.random.fold_in(jax.random.fold_in(stream_key, 6), position), (blocks,), jnp.float32, least / len(cuts), largest / len(cuts))
        level = level * jnp.repeat(jnp.exp(heights), dims[position] // blocks).reshape((-1,) + (1,) * (len(dims) - 1 - position))
    return level


def centred(stream_key, extent, scale, most, cuts=(), kind=jnp.bfloat16):
    entries = jax.random.normal(stream_key, extent, jnp.float32) * scale
    if len(cuts) > 0:
        entries = shard_levels(stream_key, extent, cuts, -0.22, 0.18) * entries
    return jnp.clip(entries, min=-most, max=most).astype(kind)


def setup_inputs(seed: int = 0) -> dict:
    key_of = jax.random.split(jax.random.key(seed), 5)
    features = centred(key_of[0], (C1, NY, PLANES, NX), 1.0, 6.0, ((1, 64), (3, 8)))
    cotangent = centred(key_of[1], (C1, NY, PLANES, NX), 1.0, 6.0, ((1, 64), (3, 8)))
    coarse_weight = centred(key_of[2], (C2, C1, 3, 3, 3), (27 * C1) ** -0.5, 0.3125)
    fine_weight = centred(key_of[3], (C1, C1 + C2, 3, 3, 3), (27 * (C1 + C2)) ** -0.5, 0.15625)
    return dict(features=features, cotangent=cotangent, coarse_weight=coarse_weight, fine_weight=fine_weight)


def pad_all(field):
    return jnp.pad(field, ((0, 0), (1, 1), (1, 1), (1, 1)))

def correlate(padded, kernel):
    result = lax.conv_general_dilated(padded[None].astype(jnp.float32), kernel.astype(jnp.float32), (1, 1, 1), 'VALID', dimension_numbers=('NCHWD', 'OIHWD', 'NCHWD'), precision=lax.Precision.HIGHEST)
    return result[0]

def flipped(kernel):
    return jnp.transpose(kernel[:, :, ::-1, ::-1, ::-1], (1, 0, 2, 3, 4))

def pool_sum(field):
    chans, rows, planes, cols = field.shape
    return field.reshape(chans, rows // 2, 2, planes // 2, 2, cols // 2, 2).sum(axis=(2, 4, 6))

def upsample(field):
    chans, rows, planes, cols = field.shape
    spread = jnp.broadcast_to(field[:, :, None, :, None, :, None], (chans, rows, 2, planes, 2, cols, 2))
    return spread.reshape(chans, 2 * rows, 2 * planes, 2 * cols)

def silu_slope(value):
    sig = jax.nn.sigmoid(value)
    return sig * (1.0 + value * (1.0 - sig))

def weight_grad(padded, grad):
    outs, rows, planes, cols = grad.shape
    grad_wide = grad.astype(jnp.float32)
    pieces = []
    for off_y in range(3):
        for off_z in range(3):
            for off_x in range(3):
                window = padded[:, off_y:off_y + rows, off_z:off_z + planes, off_x:off_x + cols].astype(jnp.float32)
                pieces.append(jnp.einsum('oyzx,cyzx->oc', grad_wide, window, precision=lax.Precision.HIGHEST))
    stacked = jnp.stack(pieces, -1)
    return stacked.reshape(outs, padded.shape[0], 3, 3, 3)

def reference(features, cotangent, coarse_weight, fine_weight):
    pooled = (pool_sum(features.astype(jnp.float32)) / 8.0).astype(jnp.bfloat16)
    pooled_pad = pad_all(pooled)
    coarse_pre = correlate(pooled_pad, coarse_weight)
    coarse_act = jax.nn.silu(coarse_pre).astype(jnp.bfloat16)
    upsampled = upsample(coarse_act)
    joined_pad = pad_all(jnp.concatenate([features, upsampled], 0))
    output = correlate(joined_pad, fine_weight).astype(jnp.bfloat16)
    grad_fine = weight_grad(joined_pad, cotangent) / math.sqrt(CELLS)
    grad_joined = correlate(pad_all(cotangent), flipped(fine_weight))
    grad_act = pool_sum(grad_joined[C1:]).astype(jnp.bfloat16)
    grad_pre = (grad_act.astype(jnp.float32) * silu_slope(coarse_pre)).astype(jnp.bfloat16)
    grad_coarse = weight_grad(pooled_pad, grad_pre) / math.sqrt(CELLS // 8)
    grad_pooled = correlate(pad_all(grad_pre), flipped(coarse_weight)).astype(jnp.bfloat16)
    grad_features = (grad_joined[:C1] + upsample(grad_pooled).astype(jnp.float32) / 8.0).astype(jnp.bfloat16)
    return (output, grad_features, grad_fine, grad_coarse)
```

```python
import functools
import math

import jax
import jax.numpy as jnp
from jax import lax
from jax.experimental import pallas as pl
from jax.experimental.pallas import tpu as pltpu
from jax.sharding import PartitionSpec as P

F32, BF16 = jnp.float32, jnp.bfloat16
MESH = pl.DeviceIdType.MESH
VMEM = pltpu.VMEM
OUTER = 4
ROWS = 192


def dot(a, b):
    return lax.dot_general(a, b, (((1,), (0,)), ((), ())), preferred_element_type=F32)


def dot_nt(a, b):
    return lax.dot_general(a, b, (((1,), (1,)), ((), ())), preferred_element_type=F32)


def iota(shape, axis):
    return lax.broadcasted_iota(jnp.int32, shape, axis)


def halo_kernel(n_wide, n_narrow, f_ref, c_ref, ext_ref, left_ref, right_ref,
                wide32, go_left, go_right, send, recv):
    me_y, me_x = lax.axis_index("wide"), lax.axis_index("narrow")
    up, down = lax.rem(me_y + n_wide - 1, n_wide), lax.rem(me_y + 1, n_wide)
    west, east = lax.rem(me_x + n_narrow - 1, n_narrow), lax.rem(me_x + 1, n_narrow)
    near = [(up, me_x), (down, me_x), (me_y, west), (me_y, east),
            (up, west), (up, east), (down, west), (down, east)]
    barrier = pltpu.get_barrier_semaphore()
    for device in near:
        pl.semaphore_signal(barrier, inc=1, device_id=device, device_id_type=MESH)
    for k, ref in enumerate((f_ref, c_ref)):
        wide32[k] = ref[...].astype(F32)
        for j in range(32):
            part = wide32[k, pl.ds(j, 16, stride=32), :]
            ext_ref[k, 128 + 16 * j:144 + 16 * j, :] = part.astype(BF16)
    row, col = iota((16, 128), 0), iota((16, 128), 1)
    for start, buf in ((0, go_left), (124, go_right)):
        total = jnp.zeros((16, 512), F32)
        for k in range(2):
            pick = (row >= 4 * k) & (row < 4 * k + 4) & (col == start + row - 4 * k)
            total += dot_nt(pick.astype(F32).astype(BF16), ext_ref[k, 128:640, :])
        buf[...] = total.astype(BF16)
    pl.semaphore_wait(barrier, 8)
    plan = [
        (ext_ref.at[:, pl.ds(128, 128), :], ext_ref.at[:, pl.ds(640, 128), :]),
        (ext_ref.at[:, pl.ds(512, 128), :], ext_ref.at[:, pl.ds(0, 128), :]),
        (go_left, right_ref.at[:, pl.ds(128, 512)]),
        (go_right, left_ref.at[:, pl.ds(128, 512)]),
        (go_left.at[:, pl.ds(0, 128)], right_ref.at[:, pl.ds(640, 128)]),
        (go_right.at[:, pl.ds(0, 128)], left_ref.at[:, pl.ds(640, 128)]),
        (go_left.at[:, pl.ds(384, 128)], right_ref.at[:, pl.ds(0, 128)]),
        (go_right.at[:, pl.ds(384, 128)], left_ref.at[:, pl.ds(0, 128)]),
    ]
    copies = []
    for j, (src, dst) in enumerate(plan):
        copies.append(pltpu.make_async_remote_copy(
            src_ref=src, dst_ref=dst, send_sem=send.at[j], recv_sem=recv.at[j],
            device_id=near[j], device_id_type=MESH))
        copies[-1].start()
    for copy in copies:
        copy.wait()


def prepare_weights(fw_ref, cw_ref, wide_w, stack, w_fwd, w_bwd, stack_c, w_pre, w_gp):
    lane = iota((16, 128), 1)
    wide_w[...] = jnp.zeros_like(wide_w)
    wide_w[0:432, 0:48] = fw_ref[...].astype(F32)
    wide_w[432:864, 0:32] = cw_ref[...].astype(F32)

    def tap(ky, kz, kx):
        at = ((ky * 3 + kz) * 3 + kx) * 16
        return wide_w[at:at + 16, :]

    zero16 = jnp.zeros((16, 128), BF16)
    for z in range(2):
        for ky in range(3):
            base = jnp.zeros((16, 128), F32)
            for kx in range(3):
                for zz in range(2):
                    at = 32 * kx + 16 * zz
                    moved = tap(ky, zz - z + 1, kx)
                    if at:
                        moved = pltpu.roll(moved, at, 1)
                    base = jnp.where((lane >= at) & (lane < at + 16), moved, base)
            for px in range(2):
                block = (pltpu.roll(base, 32, 1) if px else base).astype(BF16)
                for py in range(2):
                    rows = (py * 2 + px) * 32 + z * 16
                    w_fwd[rows:rows + 16, (ky + py) * 128:(ky + py + 1) * 128] = block
    for py in range(2):
        idle = 3 if py == 0 else 0
        for blocks in range(4):
            rows = py * 64 + blocks * 16
            w_fwd[rows:rows + 16, idle * 128:(idle + 1) * 128] = zero16
    spans = {(0, 0): (0,), (0, 1): (1, 2), (0, 2): (), (1, 0): (), (1, 1): (0, 1), (1, 2): (2,)}
    for z in range(2):
        pair = [[tap(ky, 1 - z, kx) + tap(ky, 2 - z, kx) for kx in range(3)] for ky in range(3)]
        for py in range(2):
            for dy in range(3):
                kys = spans[py, dy]
                for px in range(2):
                    rows = (py * 2 + px) * 32 + z * 16
                    block = jnp.zeros((16, 128), F32)
                    for dx in range(3):
                        terms = [pair[ky][kx] for ky in kys for kx in spans[px, dx]]
                        if not terms:
                            continue
                        moved = pltpu.roll(functools.reduce(jnp.add, terms), (32 * dx - 16) % 128, 1)
                        block = jnp.where((lane >= 32 * dx) & (lane < 32 * dx + 32), moved, block)
                    w_fwd[rows:rows + 16, 512 + dy * 128:512 + (dy + 1) * 128] = block.astype(BF16)
    for z in range(2):
        for ky in range(3):
            for wx in range(4):
                for zz in range(2):
                    at = (z * 3 + ky) * 128 + wx * 32 + zz * 16
                    if wx == 3:
                        stack[at:at + 16, :] = zero16
                    else:
                        stack[at:at + 16, :] = tap(2 - ky, 1 + z - zz, 2 - wx).astype(BF16)
    eye = (iota((48, 128), 0) == iota((48, 128), 1)).astype(F32).astype(BF16)
    turned = dot_nt(eye, stack[...])
    w_bwd[...] = jnp.zeros_like(w_bwd)
    act = [jnp.zeros((32, 128), F32) for _ in range(4)]
    for z in range(2):
        for ky in range(3):
            at = (z * 3 + ky) * 128
            base = turned[:, at:at + 128]
            for px in range(2):
                moved = pltpu.roll(base, 32, 1) if px else base
                for py in range(2):
                    rows = (py * 2 + px) * 32 + z * 16
                    w_bwd[rows:rows + 16, (ky + py) * 128:(ky + py + 1) * 128] = moved[0:16].astype(BF16)
                    act[ky + py] = act[ky + py] + moved[16:48]
    for wy in range(4):
        w_bwd[128:160, wy * 128:(wy + 1) * 128] = act[wy].astype(BF16)
    for dy in range(3):
        block = jnp.zeros((16, 128), F32)
        for dx in range(3):
            at = 432 + ((dy * 3 + 1) * 3 + dx) * 16
            stack_c[(dy * 3 + dx) * 16:(dy * 3 + dx + 1) * 16, :] = wide_w[at:at + 16, :].astype(BF16)
            at = 432 + (((2 - dy) * 3 + 1) * 3 + 2 - dx) * 16
            moved = wide_w[at:at + 16, :]
            if dx:
                moved = pltpu.roll(moved, 32 * dx, 1)
            block = jnp.where((lane >= 32 * dx) & (lane < 32 * dx + 32), moved, block)
        w_gp[:, dy * 128:(dy + 1) * 128] = block.astype(BF16)
    w_pre[...] = dot_nt(eye[0:32], stack_c[...]).astype(BF16)


def level_kernel(n_wide, n_narrow, ext_ref, left_ref, right_ref, fw_ref, cw_ref,
                 out_ref, gf_ref, sums_ref,
                 wide_w, stack, w_fwd, w_bwd, stack_c, w_pre, w_gp,
                 fine, cot, pool, act, gpre, keep_gj, flat, turn, sums):
    me_y, me_x = lax.axis_index("wide"), lax.axis_index("narrow")
    prepare_weights(fw_ref, cw_ref, wide_w, stack, w_fwd, w_bwd, stack_c, w_pre, w_gp)
    top, bottom = me_y > 0, me_y < n_wide - 1
    first, last = me_x > 0, me_x < n_narrow - 1

    want = iota((128, 512), 1)
    want = 2 * ((want & 127) - 2) - 1 + (want >> 7)
    spread = (iota((128, 512), 0) == want).astype(F32).astype(BF16)
    side_want = iota((32, 512), 1)
    side_want = 2 * ((side_want & 127) - 2) - 1 + (side_want >> 7)
    side_row = iota((32, 512), 0)
    sides = jnp.concatenate([left_ref[...].astype(F32), right_ref[...].astype(F32)], axis=0)
    turned = jnp.transpose(sides).astype(BF16)
    for k, field in enumerate((fine, cot)):
        west = (side_row >= 4 * k) & (side_row < 4 * k + 4) & (side_want == side_row - 4 * k - 4) & first
        east = (side_row >= 16 + 4 * k) & (side_row < 20 + 4 * k) & (side_want == side_row - 16 - 4 * k + 128) & last
        spread_side = (west | east).astype(F32).astype(BF16)
        for part in range(6):
            at = part * 128
            got = dot(ext_ref[k, at:at + 128, :], spread) + dot(turned[at:at + 128, :], spread_side)
            if part == 0:
                got = jnp.where(top, got, 0.0)
            if part == 5:
                got = jnp.where(bottom, got, 0.0)
            got = got.astype(BF16)
            for y in range(4):
                for wx in range(4):
                    to = (part * 4 + y) * 128 + wx * 32
                    field[to:to + 32, :] = got[y * 32:y * 32 + 32, wx * 128:wx * 128 + 128]

    for r in range(12):
        both = (fine[2 * r * 128 + 32:2 * r * 128 + 96, :].astype(F32)
                + fine[(2 * r + 1) * 128 + 32:(2 * r + 1) * 128 + 96, :].astype(F32))
        mean = (both[0:16] + both[16:32] + both[32:48] + both[48:64]) * 0.125
        pool[r * 48:r * 48 + 16, :] = pltpu.roll(mean, 1, 1).astype(BF16)
        pool[r * 48 + 16:r * 48 + 32, :] = mean.astype(BF16)
        pool[r * 48 + 32:r * 48 + 48, :] = pltpu.roll(mean, 127, 1).astype(BF16)

    lane = iota((32, 128), 1)
    inside = ((lane >= 2) | ((lane == 1) & first)) & ((lane <= 65) | ((lane == 66) & last))
    own = (iota((128, 128), 1) >= 2) & (iota((128, 128), 1) <= 65)
    blank = jnp.zeros((32, 128), BF16)
    for r in range(1, 11):
        pre = dot(w_pre[...], pool[(r - 1) * 48:(r + 2) * 48, :])
        sig = 1.0 / (1.0 + jnp.exp(-pre))
        back = dot(w_bwd[...], cot[(2 * r - 1) * 128:(2 * r + 3) * 128, :])
        grad_act = back[128:160].astype(BF16).astype(F32)
        slope = grad_act * (sig * (1.0 + pre * (1.0 - sig)))
        valid = inside
        if r == 1:
            valid = inside & top
        if r == 10:
            valid = inside & bottom
        for value, to in ((pre * sig, act), (slope, gpre)):
            value = jnp.where(valid, value, 0.0)
            at = (r - 1) * 128
            to[at:at + 32, :] = pltpu.roll(value, 1, 1).astype(BF16)
            to[at + 32:at + 64, :] = value.astype(BF16)
            to[at + 64:at + 96, :] = pltpu.roll(value, 127, 1).astype(BF16)
            to[at + 96:at + 128, :] = blank
        if 2 <= r <= 9:
            keep_gj[(r - 2) * 128:(r - 1) * 128, :] = back[0:128]

    def own_cot(r):
        a, b = 2 * r * 128, (2 * r + 1) * 128
        both = jnp.concatenate([cot[a + 32:a + 96, :], cot[b + 32:b + 96, :]], axis=0)
        return jnp.where(own, both.astype(F32), 0.0).astype(BF16)

    def lanes(parts):
        return jnp.concatenate(parts, axis=1)

    grad = jnp.zeros((128, 512), F32)
    grad_up = jnp.zeros((128, 384), F32)
    grad_c = jnp.zeros((144, 32), F32)
    for r in range(2, 10, 2):
        lhs = lanes([own_cot(r), own_cot(r + 1)])
        grad += dot_nt(lhs, lanes([fine[(2 * q - 1) * 128:(2 * q + 3) * 128, :] for q in (r, r + 1)]))
        grad_up += dot_nt(lhs, lanes([act[(q - 2) * 128:(q + 1) * 128, :] for q in (r, r + 1)]))
        mine = [jnp.where(own[0:32], gpre[(q - 1) * 128 + 32:(q - 1) * 128 + 64, :].astype(F32), 0.0).astype(BF16)
                for q in (r, r + 1)]
        grad_c += dot_nt(lanes([pool[(q - 1) * 48:(q + 2) * 48, :] for q in (r, r + 1)]), lanes(mine))
    dys = ((0, 1, 1), (1, 1, 2))
    taps = [jnp.concatenate([grad_c[t * 16:t * 16 + 16], jnp.zeros((16, 96), F32)], axis=1) for t in range(9)]
    none = jnp.zeros((16, 128), F32)
    for block in range(6):
        if block < 3:
            ky = block
            total = sum(grad[py * 64:py * 64 + 32, (ky + py) * 128:(ky + py + 1) * 128] for py in range(2))
            odd = sum(grad[py * 64 + 32:py * 64 + 64, (ky + py) * 128:(ky + py + 1) * 128] for py in range(2))
            total = total + pltpu.roll(odd, 96, 1)
        else:
            ky = block - 3
            even, odd = (sum(grad_up[py * 64 + px * 32:py * 64 + px * 32 + 32, dys[py][ky] * 128:(dys[py][ky] + 1) * 128]
                             for py in range(2)) for px in range(2))
            total = jnp.where(lane < 64, even, pltpu.roll(even, 32, 1)) + jnp.where(lane < 32, pltpu.roll(odd, 96, 1), odd)
        extra = jnp.concatenate([taps[t] if t < 9 else none for t in (2 * block, 2 * block + 1)], axis=0)
        sums[block * 32:block * 32 + 32, :] = jnp.where(lane < 96, total, pltpu.roll(extra, 96, 1))
    count, depth = sums_ref.shape[0], sums_ref.shape[1]
    for j in range(count):
        sums_ref[j] = sums[j * depth:(j + 1) * depth, :]

    joiner = iota((256, 128), 0)
    joiner = (2 * ((joiner & 127) - 2) + (joiner >> 7) == iota((256, 128), 1)).astype(F32).astype(BF16)

    def place(values, r):
        values = values.astype(BF16)
        for py in range(2):
            at = (2 * (r - 2) + py) * 32
            flat[at:at + 32, 0:128] = values[py * 64:py * 64 + 32]
            flat[at:at + 32, 128:256] = values[py * 64 + 32:py * 64 + 64]

    def finish(to):
        for part in range(4):
            joined = dot(flat[part * 128:part * 128 + 128, :], joiner)
            for j in range(8):
                turn[pl.ds(part * 8 + j, 16, stride=32), :] = joined[j * 16:j * 16 + 16]
        to[...] = turn[...].astype(BF16)

    for r in range(2, 10):
        got = dot(w_fwd[:, 0:512], fine[(2 * r - 1) * 128:(2 * r + 3) * 128, :])
        got += dot(w_fwd[:, 512:896], act[(r - 2) * 128:(r + 1) * 128, :])
        place(got, r)
    finish(out_ref)
    for r in range(2, 10):
        low = dot(w_gp[...], gpre[(r - 2) * 128:(r + 1) * 128, :]).astype(BF16).astype(F32) * 0.125
        place(keep_gj[(r - 2) * 128:(r - 1) * 128, :] + jnp.concatenate([low] * 8, axis=0), r)
    finish(gf_ref)


def sum_kernel(n_wide, n_narrow, scale_fine, scale_coarse, sums_ref, gfine_ref, gcoarse_ref,
               got1, part, got2, fin, turn, send1, recv1, send2, recv2, send3, recv3):
    g1, g2 = n_narrow * OUTER, n_wide // OUTER
    depth = ROWS // g1
    me_y, me_x = lax.axis_index("wide"), lax.axis_index("narrow")
    me1 = lax.div(me_y, g2) * n_narrow + me_x
    me2 = lax.rem(me_y, g2)

    def first(k):
        return (lax.div(k, n_narrow) * g2 + me2, lax.rem(k, n_narrow))

    def second(k):
        return (lax.div(me_y, g2) * g2 + k, me_x)

    barrier = pltpu.get_barrier_semaphore()

    @pl.loop(1, g1)
    def _(d):
        pl.semaphore_signal(barrier, inc=1, device_id=first(lax.rem(me1 + d, g1)), device_id_type=MESH)

    @pl.loop(1, g2)
    def _(d):
        pl.semaphore_signal(barrier, inc=1, device_id=second(lax.rem(me2 + d, g2)), device_id_type=MESH)

    pl.semaphore_wait(barrier, g1 + g2 - 2)

    def copy1(d):
        to = lax.rem(me1 + d, g1)
        return pltpu.make_async_remote_copy(
            src_ref=sums_ref.at[to], dst_ref=got1.at[d], send_sem=send1.at[d], recv_sem=recv1.at[d],
            device_id=first(to), device_id_type=MESH)

    def copy2(d, slot):
        return pltpu.make_async_remote_copy(
            src_ref=part, dst_ref=got2.at[slot], send_sem=send2.at[d], recv_sem=recv2.at[slot],
            device_id=second(lax.rem(me2 + d, g2)), device_id_type=MESH)

    def copy3(d, slot):
        return pltpu.make_async_remote_copy(
            src_ref=fin.at[me1], dst_ref=fin.at[slot], send_sem=send3.at[d], recv_sem=recv3.at[slot],
            device_id=first(lax.rem(me1 + d, g1)), device_id_type=MESH)

    def run(count, body):
        @pl.loop(1, count)
        def _(d):
            body(d)

    run(g1, lambda d: copy1(d).start())
    run(g1, lambda d: copy1(d).wait_recv())
    total = sums_ref[me1]
    for d in range(1, g1):
        total += got1[d]
    part[...] = total
    run(g2, lambda d: copy2(d, me2).start())
    got2[me2] = total
    run(g2, lambda d: copy2(d, lax.rem(me2 + d, g2)).wait_recv())
    total = got2[0]
    for k in range(1, g2):
        total += got2[k]
    fin[me1] = total
    run(g1, lambda d: copy3(d, me1).start())
    run(g1, lambda d: copy3(d, lax.rem(me1 + d, g1)).wait_recv())
    for j in range(g1):
        turn[j * depth:(j + 1) * depth, :] = fin[j]
    lane = iota((16, 128), 1)
    for ky in range(3):
        flow = [turn[ky * 32 + z * 16:ky * 32 + z * 16 + 16, :] for z in range(2)]
        rise = [turn[96 + ky * 32 + z * 16:96 + ky * 32 + z * 16 + 16, :] for z in range(2)]
        ups = (rise[1], rise[0] + rise[1], rise[0])
        for kx in range(3):
            near0 = [pltpu.roll(flow[z], (-32 * kx) % 128, 1) if kx else flow[z] for z in range(2)]
            near1 = [pltpu.roll(flow[z], (-32 * kx - 16) % 128, 1) for z in range(2)]
            own = (near0[1], near0[0] + near1[1], near1[0])
            for kz in range(3):
                whole = jnp.where(lane < 16, own[kz], pltpu.roll(ups[kz], (16 - 32 * kx) % 128, 1))
                at = ((ky * 3 + kz) * 3 + kx) * 16
                gfine_ref[at:at + 16, :] = (whole * scale_fine)[:, 0:48]
                if kz == 1:
                    t = ky * 3 + kx
                    row = (t // 2) * 32 + (t % 2) * 16
                    coarse = pltpu.roll(turn[row:row + 16, :], 32, 1)[:, 0:32] * scale_coarse
                    gcoarse_ref[at:at + 16, :] = coarse
                else:
                    gcoarse_ref[at:at + 16, :] = jnp.zeros((16, 32), F32)
    run(g1, lambda d: copy1(d).wait_send())
    run(g2, lambda d: copy2(d, me2).wait_send())
    run(g1, lambda d: copy3(d, me1).wait_send())


def shards(n_wide, n_narrow, features, cotangent, coarse_weight, fine_weight):
    inside = pl.BlockSpec(memory_space=VMEM)
    shape = jax.ShapeDtypeStruct
    g1, g2 = n_narrow * OUTER, n_wide // OUTER
    depth = ROWS // g1
    cells = n_wide * 16 * 2 * n_narrow * 128
    fw = jnp.transpose(fine_weight, (2, 3, 4, 0, 1)).reshape(432, 48)
    cw = jnp.transpose(coarse_weight, (2, 3, 4, 1, 0)).reshape(432, 32)
    dma = pltpu.SemaphoreType.DMA
    ext, left, right = pl.pallas_call(
        functools.partial(halo_kernel, n_wide, n_narrow),
        out_shape=(shape((2, 768, 128), BF16), shape((16, 768), BF16), shape((16, 768), BF16)),
        in_specs=[inside] * 2,
        out_specs=(inside,) * 3,
        scratch_shapes=[VMEM((2, 512, 128), F32), VMEM((16, 512), BF16), VMEM((16, 512), BF16), dma((8,)), dma((8,))],
        compiler_params=pltpu.CompilerParams(collective_id=0, has_side_effects=True),
        name="halo",
    )(features.reshape(512, 128), cotangent.reshape(512, 128))
    output, grad_features, sums = pl.pallas_call(
        functools.partial(level_kernel, n_wide, n_narrow),
        out_shape=(shape((512, 128), BF16), shape((512, 128), BF16), shape((g1, depth, 128), F32)),
        in_specs=[inside] * 5,
        out_specs=(inside,) * 3,
        scratch_shapes=[
            VMEM((864, 128), F32), VMEM((768, 128), BF16), VMEM((128, 896), BF16), VMEM((160, 512), BF16),
            VMEM((144, 128), BF16), VMEM((32, 144), BF16), VMEM((16, 384), BF16),
            VMEM((3072, 128), BF16), VMEM((3072, 128), BF16), VMEM((576, 128), BF16),
            VMEM((1280, 128), BF16), VMEM((1280, 128), BF16), VMEM((1024, 128), F32),
            VMEM((512, 256), BF16), VMEM((512, 128), F32), VMEM((ROWS, 128), F32),
        ],
        compiler_params=pltpu.CompilerParams(vmem_limit_bytes=40 * 1024 * 1024),
        name="level",
    )(ext, left, right, fw, cw)
    gfine, gcoarse = pl.pallas_call(
        functools.partial(sum_kernel, n_wide, n_narrow, 1.0 / math.sqrt(cells), 1.0 / math.sqrt(cells // 8)),
        out_shape=(shape((432, 48), F32), shape((432, 32), F32)),
        in_specs=[inside],
        out_specs=(inside,) * 2,
        scratch_shapes=[
            VMEM((g1, depth, 128), F32), VMEM((depth, 128), F32), VMEM((g2, depth, 128), F32),
            VMEM((g1, depth, 128), F32), VMEM((ROWS, 128), F32),
            dma((g1,)), dma((g1,)), dma((g2,)), dma((g2,)), dma((g1,)), dma((g1,)),
        ],
        compiler_params=pltpu.CompilerParams(collective_id=1, has_side_effects=True),
        name="sums",
    )(sums)
    return (
        output.reshape(16, 16, 2, 128),
        grad_features.reshape(16, 16, 2, 128),
        jnp.transpose(gfine.reshape(3, 3, 3, 16, 48), (3, 4, 0, 1, 2)),
        jnp.transpose(gcoarse.reshape(3, 3, 3, 16, 32), (4, 3, 0, 1, 2)),
    )


def solution(mesh):
    placed = P(None, "wide", None, "narrow")
    return jax.shard_map(
        functools.partial(shards, mesh.shape["wide"], mesh.shape["narrow"]),
        mesh=mesh,
        in_specs=(placed, placed, P(), P()),
        out_specs=(placed, placed, P(), P()),
        check_vma=False,
    )
```

```python
import functools
import math

import jax
import jax.numpy as jnp
from jax import lax
from jax.experimental import pallas as pl
from jax.experimental.pallas import tpu as pltpu
from jax.sharding import PartitionSpec as P

F32, BF16 = jnp.float32, jnp.bfloat16
MESH = pl.DeviceIdType.MESH
VMEM = pltpu.VMEM
OUTER = 4
ROWS = 192


def dot(a, b):
    return lax.dot_general(a, b, (((1,), (0,)), ((), ())), preferred_element_type=F32)


def dot_nt(a, b):
    return lax.dot_general(a, b, (((1,), (1,)), ((), ())), preferred_element_type=F32)


def iota(shape, axis):
    return lax.broadcasted_iota(jnp.int32, shape, axis)


def neighbours(n_wide, n_narrow, me_y, me_x):
    up, down = lax.rem(me_y + n_wide - 1, n_wide), lax.rem(me_y + 1, n_wide)
    west, east = lax.rem(me_x + n_narrow - 1, n_narrow), lax.rem(me_x + 1, n_narrow)
    return [(up, me_x), (down, me_x), (me_y, west), (me_y, east),
            (up, west), (up, east), (down, west), (down, east)]


def pack_own(f_ref, c_ref, ext_ref, wide32, go_left, go_right):
    for k, ref in enumerate((f_ref, c_ref)):
        wide32[k] = ref[...].astype(F32)
        for j in range(32):
            part = wide32[k, pl.ds(j, 16, stride=32), :]
            ext_ref[k, 128 + 16 * j:144 + 16 * j, :] = part.astype(BF16)
    row, col = iota((16, 128), 0), iota((16, 128), 1)
    for start, buf in ((0, go_left), (124, go_right)):
        total = jnp.zeros((16, 512), F32)
        for k in range(2):
            pick = (row >= 4 * k) & (row < 4 * k + 4) & (col == start + row - 4 * k)
            total += dot_nt(pick.astype(F32).astype(BF16), ext_ref[k, 128:640, :])
        buf[...] = total.astype(BF16)


def halo_copies(near, ext_ref, left_ref, right_ref, go_left, go_right, send, recv):
    plan = [
        (ext_ref.at[:, pl.ds(128, 128), :], ext_ref.at[:, pl.ds(640, 128), :]),
        (ext_ref.at[:, pl.ds(512, 128), :], ext_ref.at[:, pl.ds(0, 128), :]),
        (go_left, right_ref.at[:, pl.ds(128, 512)]),
        (go_right, left_ref.at[:, pl.ds(128, 512)]),
        (go_left.at[:, pl.ds(0, 128)], right_ref.at[:, pl.ds(640, 128)]),
        (go_right.at[:, pl.ds(0, 128)], left_ref.at[:, pl.ds(640, 128)]),
        (go_left.at[:, pl.ds(384, 128)], right_ref.at[:, pl.ds(0, 128)]),
        (go_right.at[:, pl.ds(384, 128)], left_ref.at[:, pl.ds(0, 128)]),
    ]
    return [
        pltpu.make_async_remote_copy(
            src_ref=src, dst_ref=dst, send_sem=send.at[j], recv_sem=recv.at[j],
            device_id=near[j], device_id_type=MESH)
        for j, (src, dst) in enumerate(plan)
    ]


def prepare_weights(fw_ref, cw_ref, wide_w, stack, w_fwd, w_bwd, stack_c, w_pre, w_gp):
    lane = iota((16, 128), 1)
    wide_w[...] = jnp.zeros_like(wide_w)
    wide_w[0:432, 0:48] = fw_ref[...].astype(F32)
    wide_w[432:864, 0:32] = cw_ref[...].astype(F32)

    def tap(ky, kz, kx):
        at = ((ky * 3 + kz) * 3 + kx) * 16
        return wide_w[at:at + 16, :]

    zero16 = jnp.zeros((16, 128), BF16)
    for z in range(2):
        for ky in range(3):
            base = jnp.zeros((16, 128), F32)
            for kx in range(3):
                for zz in range(2):
                    at = 32 * kx + 16 * zz
                    moved = tap(ky, zz - z + 1, kx)
                    if at:
                        moved = pltpu.roll(moved, at, 1)
                    base = jnp.where((lane >= at) & (lane < at + 16), moved, base)
            for px in range(2):
                block = (pltpu.roll(base, 32, 1) if px else base).astype(BF16)
                for py in range(2):
                    rows = (py * 2 + px) * 32 + z * 16
                    w_fwd[rows:rows + 16, (ky + py) * 128:(ky + py + 1) * 128] = block
    for py in range(2):
        idle = 3 if py == 0 else 0
        for blocks in range(4):
            rows = py * 64 + blocks * 16
            w_fwd[rows:rows + 16, idle * 128:(idle + 1) * 128] = zero16
    spans = {(0, 0): (0,), (0, 1): (1, 2), (0, 2): (), (1, 0): (), (1, 1): (0, 1), (1, 2): (2,)}
    for z in range(2):
        pair = [[tap(ky, 1 - z, kx) + tap(ky, 2 - z, kx) for kx in range(3)] for ky in range(3)]
        for py in range(2):
            for dy in range(3):
                kys = spans[py, dy]
                for px in range(2):
                    rows = (py * 2 + px) * 32 + z * 16
                    block = jnp.zeros((16, 128), F32)
                    for dx in range(3):
                        terms = [pair[ky][kx] for ky in kys for kx in spans[px, dx]]
                        if not terms:
                            continue
                        moved = pltpu.roll(functools.reduce(jnp.add, terms), (32 * dx - 16) % 128, 1)
                        block = jnp.where((lane >= 32 * dx) & (lane < 32 * dx + 32), moved, block)
                    w_fwd[rows:rows + 16, 512 + dy * 128:512 + (dy + 1) * 128] = block.astype(BF16)
    for z in range(2):
        for ky in range(3):
            for wx in range(4):
                for zz in range(2):
                    at = (z * 3 + ky) * 128 + wx * 32 + zz * 16
                    if wx == 3:
                        stack[at:at + 16, :] = zero16
                    else:
                        stack[at:at + 16, :] = tap(2 - ky, 1 + z - zz, 2 - wx).astype(BF16)
    eye = (iota((48, 128), 0) == iota((48, 128), 1)).astype(F32).astype(BF16)
    turned = dot_nt(eye, stack[...])
    w_bwd[...] = jnp.zeros_like(w_bwd)
    act = [jnp.zeros((32, 128), F32) for _ in range(4)]
    for z in range(2):
        for ky in range(3):
            at = (z * 3 + ky) * 128
            base = turned[:, at:at + 128]
            for px in range(2):
                moved = pltpu.roll(base, 32, 1) if px else base
                for py in range(2):
                    rows = (py * 2 + px) * 32 + z * 16
                    w_bwd[rows:rows + 16, (ky + py) * 128:(ky + py + 1) * 128] = moved[0:16].astype(BF16)
                    act[ky + py] = act[ky + py] + moved[16:48]
    for wy in range(4):
        w_bwd[128:160, wy * 128:(wy + 1) * 128] = act[wy].astype(BF16)
    for dy in range(3):
        block = jnp.zeros((16, 128), F32)
        for dx in range(3):
            at = 432 + ((dy * 3 + 1) * 3 + dx) * 16
            stack_c[(dy * 3 + dx) * 16:(dy * 3 + dx + 1) * 16, :] = wide_w[at:at + 16, :].astype(BF16)
            at = 432 + (((2 - dy) * 3 + 1) * 3 + 2 - dx) * 16
            moved = wide_w[at:at + 16, :]
            if dx:
                moved = pltpu.roll(moved, 32 * dx, 1)
            block = jnp.where((lane >= 32 * dx) & (lane < 32 * dx + 32), moved, block)
        w_gp[:, dy * 128:(dy + 1) * 128] = block.astype(BF16)
    w_pre[...] = dot_nt(eye[0:32], stack_c[...]).astype(BF16)


def level_gradients(n_wide, n_narrow, me_y, me_x, ext_ref, left_ref, right_ref, sums_ref,
                    w_bwd, w_pre, fine, cot, pool, act, gpre, keep_gj, sums):
    top, bottom = me_y > 0, me_y < n_wide - 1
    first, last = me_x > 0, me_x < n_narrow - 1

    want = iota((128, 512), 1)
    want = 2 * ((want & 127) - 2) - 1 + (want >> 7)
    spread = (iota((128, 512), 0) == want).astype(F32).astype(BF16)
    side_want = iota((32, 512), 1)
    side_want = 2 * ((side_want & 127) - 2) - 1 + (side_want >> 7)
    side_row = iota((32, 512), 0)
    sides = jnp.concatenate([left_ref[...].astype(F32), right_ref[...].astype(F32)], axis=0)
    turned = jnp.transpose(sides).astype(BF16)
    for k, field in enumerate((fine, cot)):
        west = (side_row >= 4 * k) & (side_row < 4 * k + 4) & (side_want == side_row - 4 * k - 4) & first
        east = (side_row >= 16 + 4 * k) & (side_row < 20 + 4 * k) & (side_want == side_row - 16 - 4 * k + 128) & last
        spread_side = (west | east).astype(F32).astype(BF16)
        for part in range(6):
            at = part * 128
            got = dot(ext_ref[k, at:at + 128, :], spread) + dot(turned[at:at + 128, :], spread_side)
            if part == 0:
                got = jnp.where(top, got, 0.0)
            if part == 5:
                got = jnp.where(bottom, got, 0.0)
            got = got.astype(BF16)
            for y in range(4):
                for wx in range(4):
                    to = (part * 4 + y) * 128 + wx * 32
                    field[to:to + 32, :] = got[y * 32:y * 32 + 32, wx * 128:wx * 128 + 128]

    for r in range(12):
        both = (fine[2 * r * 128 + 32:2 * r * 128 + 96, :].astype(F32)
                + fine[(2 * r + 1) * 128 + 32:(2 * r + 1) * 128 + 96, :].astype(F32))
        mean = (both[0:16] + both[16:32] + both[32:48] + both[48:64]) * 0.125
        pool[r * 48:r * 48 + 16, :] = pltpu.roll(mean, 1, 1).astype(BF16)
        pool[r * 48 + 16:r * 48 + 32, :] = mean.astype(BF16)
        pool[r * 48 + 32:r * 48 + 48, :] = pltpu.roll(mean, 127, 1).astype(BF16)

    lane = iota((32, 128), 1)
    inside = ((lane >= 2) | ((lane == 1) & first)) & ((lane <= 65) | ((lane == 66) & last))
    own = (iota((128, 128), 1) >= 2) & (iota((128, 128), 1) <= 65)
    blank = jnp.zeros((32, 128), BF16)
    for r in range(1, 11):
        pre = dot(w_pre[...], pool[(r - 1) * 48:(r + 2) * 48, :])
        sig = 1.0 / (1.0 + jnp.exp(-pre))
        back = dot(w_bwd[...], cot[(2 * r - 1) * 128:(2 * r + 3) * 128, :])
        grad_act = back[128:160].astype(BF16).astype(F32)
        slope = grad_act * (sig * (1.0 + pre * (1.0 - sig)))
        valid = inside
        if r == 1:
            valid = inside & top
        if r == 10:
            valid = inside & bottom
        for value, to in ((pre * sig, act), (slope, gpre)):
            value = jnp.where(valid, value, 0.0)
            at = (r - 1) * 128
            to[at:at + 32, :] = pltpu.roll(value, 1, 1).astype(BF16)
            to[at + 32:at + 64, :] = value.astype(BF16)
            to[at + 64:at + 96, :] = pltpu.roll(value, 127, 1).astype(BF16)
            to[at + 96:at + 128, :] = blank
        if 2 <= r <= 9:
            keep_gj[(r - 2) * 128:(r - 1) * 128, :] = back[0:128]

    def own_cot(r):
        a, b = 2 * r * 128, (2 * r + 1) * 128
        both = jnp.concatenate([cot[a + 32:a + 96, :], cot[b + 32:b + 96, :]], axis=0)
        return jnp.where(own, both.astype(F32), 0.0).astype(BF16)

    def lanes(parts):
        return jnp.concatenate(parts, axis=1)

    grad = jnp.zeros((128, 512), F32)
    grad_up = jnp.zeros((128, 384), F32)
    grad_c = jnp.zeros((144, 32), F32)
    for r in range(2, 10, 2):
        lhs = lanes([own_cot(r), own_cot(r + 1)])
        grad += dot_nt(lhs, lanes([fine[(2 * q - 1) * 128:(2 * q + 3) * 128, :] for q in (r, r + 1)]))
        grad_up += dot_nt(lhs, lanes([act[(q - 2) * 128:(q + 1) * 128, :] for q in (r, r + 1)]))
        mine = [jnp.where(own[0:32], gpre[(q - 1) * 128 + 32:(q - 1) * 128 + 64, :].astype(F32), 0.0).astype(BF16)
                for q in (r, r + 1)]
        grad_c += dot_nt(lanes([pool[(q - 1) * 48:(q + 2) * 48, :] for q in (r, r + 1)]), lanes(mine))
    dys = ((0, 1, 1), (1, 1, 2))
    taps = [jnp.concatenate([grad_c[t * 16:t * 16 + 16], jnp.zeros((16, 96), F32)], axis=1) for t in range(9)]
    none = jnp.zeros((16, 128), F32)
    for block in range(6):
        if block < 3:
            ky = block
            total = sum(grad[py * 64:py * 64 + 32, (ky + py) * 128:(ky + py + 1) * 128] for py in range(2))
            odd = sum(grad[py * 64 + 32:py * 64 + 64, (ky + py) * 128:(ky + py + 1) * 128] for py in range(2))
            total = total + pltpu.roll(odd, 96, 1)
        else:
            ky = block - 3
            even, odd = (sum(grad_up[py * 64 + px * 32:py * 64 + px * 32 + 32, dys[py][ky] * 128:(dys[py][ky] + 1) * 128]
                             for py in range(2)) for px in range(2))
            total = jnp.where(lane < 64, even, pltpu.roll(even, 32, 1)) + jnp.where(lane < 32, pltpu.roll(odd, 96, 1), odd)
        extra = jnp.concatenate([taps[t] if t < 9 else none for t in (2 * block, 2 * block + 1)], axis=0)
        sums[block * 32:block * 32 + 32, :] = jnp.where(lane < 96, total, pltpu.roll(extra, 96, 1))
    count, depth = sums_ref.shape[0], sums_ref.shape[1]
    for j in range(count):
        sums_ref[j] = sums[j * depth:(j + 1) * depth, :]


def level_outputs(out_ref, gf_ref, w_fwd, w_gp, fine, act, gpre, keep_gj, flat, turn):
    joiner = iota((256, 128), 0)
    joiner = (2 * ((joiner & 127) - 2) + (joiner >> 7) == iota((256, 128), 1)).astype(F32).astype(BF16)

    def place(values, r):
        values = values.astype(BF16)
        for py in range(2):
            at = (2 * (r - 2) + py) * 32
            flat[at:at + 32, 0:128] = values[py * 64:py * 64 + 32]
            flat[at:at + 32, 128:256] = values[py * 64 + 32:py * 64 + 64]

    def finish(to):
        for part in range(4):
            joined = dot(flat[part * 128:part * 128 + 128, :], joiner)
            for j in range(8):
                turn[pl.ds(part * 8 + j, 16, stride=32), :] = joined[j * 16:j * 16 + 16]
        to[...] = turn[...].astype(BF16)

    for r in range(2, 10):
        got = dot(w_fwd[:, 0:512], fine[(2 * r - 1) * 128:(2 * r + 3) * 128, :])
        got += dot(w_fwd[:, 512:896], act[(r - 2) * 128:(r + 1) * 128, :])
        place(got, r)
    finish(out_ref)
    for r in range(2, 10):
        low = dot(w_gp[...], gpre[(r - 2) * 128:(r + 1) * 128, :]).astype(BF16).astype(F32) * 0.125
        place(keep_gj[(r - 2) * 128:(r - 1) * 128, :] + jnp.concatenate([low] * 8, axis=0), r)
    finish(gf_ref)


def main_kernel(n_wide, n_narrow, f_ref, c_ref, fw_ref, cw_ref, out_hbm, gf_hbm, total_ref,
                wide32, go_left, go_right, ext, left, right, halo_send, halo_recv,
                wide_w, stack, w_fwd, w_bwd, stack_c, w_pre, w_gp,
                fine, cot, pool, act, gpre, keep_gj, flat, turn, sums,
                out_v, gf_v, out_sem, mine, got1, part, got2, fin, send1, recv1, send2, recv2, send3, recv3):
    g1, g2 = n_wide // OUTER, n_narrow * OUTER
    depth = ROWS // g1
    me_y, me_x = lax.axis_index("wide"), lax.axis_index("narrow")
    me1 = lax.rem(me_y, g1)
    me2 = lax.div(me_y, g1) * n_narrow + me_x

    def first(k):
        return (me_y - me1 + k, me_x)

    def second(k):
        return (lax.div(k, n_narrow) * g1 + me1, lax.rem(k, n_narrow))

    def run(count, body):
        @pl.loop(1, count)
        def _(d):
            body(d)

    barrier = pltpu.get_barrier_semaphore()
    near = neighbours(n_wide, n_narrow, me_y, me_x)

    def greet(device):
        pl.semaphore_signal(barrier, inc=1, device_id=device, device_id_type=MESH)

    for device in near:
        greet(device)
    run(g2, lambda d: greet(second(lax.rem(me2 + d, g2))))
    run(g1, lambda d: greet(first(lax.rem(me1 + d, g1))))
    pack_own(f_ref, c_ref, ext, wide32, go_left, go_right)
    prepare_weights(fw_ref, cw_ref, wide_w, stack, w_fwd, w_bwd, stack_c, w_pre, w_gp)
    pl.semaphore_wait(barrier, 8 + g1 + g2 - 2)
    halo = halo_copies(near, ext, left, right, go_left, go_right, halo_send, halo_recv)
    for copy in halo:
        copy.start()
    for copy in halo:
        copy.wait_recv()
    level_gradients(n_wide, n_narrow, me_y, me_x, ext, left, right, mine,
                    w_bwd, w_pre, fine, cot, pool, act, gpre, keep_gj, sums)

    def copy1(d):
        to = lax.rem(me1 + d, g1)
        return pltpu.make_async_remote_copy(
            src_ref=mine.at[to], dst_ref=got1.at[d], send_sem=send1.at[d], recv_sem=recv1.at[d],
            device_id=first(to), device_id_type=MESH)

    def copy2(d, slot):
        return pltpu.make_async_remote_copy(
            src_ref=part, dst_ref=got2.at[slot], send_sem=send2.at[d], recv_sem=recv2.at[slot],
            device_id=second(lax.rem(me2 + d, g2)), device_id_type=MESH)

    def copy3(d, slot):
        return pltpu.make_async_remote_copy(
            src_ref=fin.at[me1], dst_ref=fin.at[slot], send_sem=send3.at[d], recv_sem=recv3.at[slot],
            device_id=first(lax.rem(me1 + d, g1)), device_id_type=MESH)

    run(g1, lambda d: copy1(d).start())
    level_outputs(out_v, gf_v, w_fwd, w_gp, fine, act, gpre, keep_gj, flat, turn)
    writes = [pltpu.make_async_copy(out_v, out_hbm, out_sem.at[0]), pltpu.make_async_copy(gf_v, gf_hbm, out_sem.at[1])]
    for write in writes:
        write.start()
    run(g1, lambda d: copy1(d).wait_recv())
    total = mine[me1]
    for d in range(1, g1):
        total += got1[d]
    part[...] = total
    run(g2, lambda d: copy2(d, me2).start())
    got2[me2] = total
    run(g2, lambda d: copy2(d, lax.rem(me2 + d, g2)).wait_recv())
    total = got2[0]
    for k in range(1, g2):
        total += got2[k]
    fin[me1] = total
    run(g1, lambda d: copy3(d, me1).start())
    for copy in halo:
        copy.wait_send()
    for write in writes:
        write.wait()
    run(g1, lambda d: copy1(d).wait_send())
    run(g2, lambda d: copy2(d, me2).wait_send())
    run(g1, lambda d: copy3(d, lax.rem(me1 + d, g1)).wait_recv())
    for j in range(g1):
        total_ref[j * depth:(j + 1) * depth, :] = fin[j]
    run(g1, lambda d: copy3(d, me1).wait_send())


def finish_kernel(scale_fine, scale_coarse, turn, out_in, gf_in, gfine_ref, gcoarse_ref, out_ref, gf_ref, sem):
    copies = [pltpu.make_async_copy(out_in, out_ref, sem.at[0]), pltpu.make_async_copy(gf_in, gf_ref, sem.at[1])]
    for copy in copies:
        copy.start()
    lane = iota((16, 128), 1)
    for ky in range(3):
        flow = [turn[ky * 32 + z * 16:ky * 32 + z * 16 + 16, :] for z in range(2)]
        rise = [turn[96 + ky * 32 + z * 16:96 + ky * 32 + z * 16 + 16, :] for z in range(2)]
        ups = (rise[1], rise[0] + rise[1], rise[0])
        for kx in range(3):
            near0 = [pltpu.roll(flow[z], (-32 * kx) % 128, 1) if kx else flow[z] for z in range(2)]
            near1 = [pltpu.roll(flow[z], (-32 * kx - 16) % 128, 1) for z in range(2)]
            own = (near0[1], near0[0] + near1[1], near1[0])
            for kz in range(3):
                whole = jnp.where(lane < 16, own[kz], pltpu.roll(ups[kz], (16 - 32 * kx) % 128, 1))
                at = ((ky * 3 + kz) * 3 + kx) * 16
                gfine_ref[at:at + 16, :] = (whole * scale_fine)[:, 0:48]
                if kz == 1:
                    t = ky * 3 + kx
                    row = (t // 2) * 32 + (t % 2) * 16
                    coarse = pltpu.roll(turn[row:row + 16, :], 32, 1)[:, 0:32] * scale_coarse
                    gcoarse_ref[at:at + 16, :] = coarse
                else:
                    gcoarse_ref[at:at + 16, :] = jnp.zeros((16, 32), F32)
    for copy in copies:
        copy.wait()


def shards(n_wide, n_narrow, features, cotangent, coarse_weight, fine_weight):
    inside = pl.BlockSpec(memory_space=VMEM)
    shape = jax.ShapeDtypeStruct
    g1, g2 = n_wide // OUTER, n_narrow * OUTER
    depth = ROWS // g1
    cells = n_wide * 16 * 2 * n_narrow * 128
    fw = jnp.transpose(fine_weight, (2, 3, 4, 0, 1)).reshape(432, 48)
    cw = jnp.transpose(coarse_weight, (2, 3, 4, 1, 0)).reshape(432, 32)
    dma = pltpu.SemaphoreType.DMA
    large = pl.BlockSpec(memory_space=pl.ANY)
    output, grad_features, sums = pl.pallas_call(
        functools.partial(main_kernel, n_wide, n_narrow),
        out_shape=(shape((512, 128), BF16), shape((512, 128), BF16), shape((ROWS, 128), F32)),
        in_specs=[inside] * 4,
        out_specs=(large, large, inside),
        scratch_shapes=[
            VMEM((2, 512, 128), F32), VMEM((16, 512), BF16), VMEM((16, 512), BF16),
            VMEM((2, 768, 128), BF16), VMEM((16, 768), BF16), VMEM((16, 768), BF16), dma((8,)), dma((8,)),
            VMEM((864, 128), F32), VMEM((768, 128), BF16), VMEM((128, 896), BF16), VMEM((160, 512), BF16),
            VMEM((144, 128), BF16), VMEM((32, 144), BF16), VMEM((16, 384), BF16),
            VMEM((3072, 128), BF16), VMEM((3072, 128), BF16), VMEM((576, 128), BF16),
            VMEM((1280, 128), BF16), VMEM((1280, 128), BF16), VMEM((1024, 128), F32),
            VMEM((512, 256), BF16), VMEM((512, 128), F32), VMEM((ROWS, 128), F32),
            VMEM((512, 128), BF16), VMEM((512, 128), BF16), dma((2,)),
            VMEM((g1, depth, 128), F32), VMEM((g1, depth, 128), F32), VMEM((depth, 128), F32),
            VMEM((g2, depth, 128), F32), VMEM((g1, depth, 128), F32),
            dma((g1,)), dma((g1,)), dma((g2,)), dma((g2,)), dma((g1,)), dma((g1,)),
        ],
        compiler_params=pltpu.CompilerParams(
            collective_id=0, has_side_effects=True, vmem_limit_bytes=40 * 1024 * 1024),
        name="levels",
    )(features.reshape(512, 128), cotangent.reshape(512, 128), fw, cw)
    gfine, gcoarse, output, grad_features = pl.pallas_call(
        functools.partial(finish_kernel, 1.0 / math.sqrt(cells), 1.0 / math.sqrt(cells // 8)),
        out_shape=(shape((432, 48), F32), shape((432, 32), F32), shape((512, 128), BF16), shape((512, 128), BF16)),
        in_specs=[inside, large, large],
        out_specs=(inside, inside, large, large),
        scratch_shapes=[dma((2,))],
        name="finish",
    )(sums, output, grad_features)
    return (
        output.reshape(16, 16, 2, 128),
        grad_features.reshape(16, 16, 2, 128),
        jnp.transpose(gfine.reshape(3, 3, 3, 16, 48), (3, 4, 0, 1, 2)),
        jnp.transpose(gcoarse.reshape(3, 3, 3, 16, 32), (4, 3, 0, 1, 2)),
    )


def solution(mesh):
    placed = P(None, "wide", None, "narrow")
    return jax.shard_map(
        functools.partial(shards, mesh.shape["wide"], mesh.shape["narrow"]),
        mesh=mesh,
        in_specs=(placed, placed, P(), P()),
        out_specs=(placed, placed, P(), P()),
        check_vma=False,
    )
```

```python
import functools
import math

import jax
import jax.numpy as jnp
from jax import lax
from jax.experimental import pallas as pl
from jax.experimental.pallas import tpu as pltpu
from jax.sharding import PartitionSpec as P

F32, BF16 = jnp.float32, jnp.bfloat16
MESH = pl.DeviceIdType.MESH
VMEM = pltpu.VMEM
OUTER = 4
ROWS = 192


def dot(a, b):
    return lax.dot_general(a, b, (((1,), (0,)), ((), ())), preferred_element_type=F32)


def dot_nt(a, b):
    return lax.dot_general(a, b, (((1,), (1,)), ((), ())), preferred_element_type=F32)


def iota(shape, axis):
    return lax.broadcasted_iota(jnp.int32, shape, axis)


def neighbours(n_wide, n_narrow, me_y, me_x):
    up, down = lax.rem(me_y + n_wide - 1, n_wide), lax.rem(me_y + 1, n_wide)
    west, east = lax.rem(me_x + n_narrow - 1, n_narrow), lax.rem(me_x + 1, n_narrow)
    return [(up, me_x), (down, me_x), (me_y, west), (me_y, east),
            (up, west), (up, east), (down, west), (down, east)]


def pack_own(f_ref, c_ref, ext_ref, wide32, go_left, go_right):
    for k, ref in enumerate((f_ref, c_ref)):
        wide32[k] = ref[...].astype(F32)
        for j in range(32):
            part = wide32[k, pl.ds(j, 16, stride=32), :]
            ext_ref[k, 128 + 16 * j:144 + 16 * j, :] = part.astype(BF16)
    row, col = iota((16, 128), 0), iota((16, 128), 1)
    for start, buf in ((0, go_left), (124, go_right)):
        total = jnp.zeros((16, 512), F32)
        for k in range(2):
            pick = (row >= 4 * k) & (row < 4 * k + 4) & (col == start + row - 4 * k)
            total += dot_nt(pick.astype(F32).astype(BF16), ext_ref[k, 128:640, :])
        buf[...] = total.astype(BF16)


def halo_copies(near, ext_ref, left_ref, right_ref, go_left, go_right, send, recv):
    plan = [
        (ext_ref.at[:, pl.ds(128, 128), :], ext_ref.at[:, pl.ds(640, 128), :]),
        (ext_ref.at[:, pl.ds(512, 128), :], ext_ref.at[:, pl.ds(0, 128), :]),
        (go_left, right_ref.at[:, pl.ds(128, 512)]),
        (go_right, left_ref.at[:, pl.ds(128, 512)]),
        (go_left.at[:, pl.ds(0, 128)], right_ref.at[:, pl.ds(640, 128)]),
        (go_right.at[:, pl.ds(0, 128)], left_ref.at[:, pl.ds(640, 128)]),
        (go_left.at[:, pl.ds(384, 128)], right_ref.at[:, pl.ds(0, 128)]),
        (go_right.at[:, pl.ds(384, 128)], left_ref.at[:, pl.ds(0, 128)]),
    ]
    return [
        pltpu.make_async_remote_copy(
            src_ref=src, dst_ref=dst, send_sem=send.at[j], recv_sem=recv.at[j],
            device_id=near[j], device_id_type=MESH)
        for j, (src, dst) in enumerate(plan)
    ]


def prepare_weights(fw_ref, cw_ref, wide_w, stack, w_fwd, w_bwd, stack_c, w_pre, w_gp):
    lane = iota((16, 128), 1)
    wide_w[...] = jnp.zeros_like(wide_w)
    wide_w[0:432, 0:48] = fw_ref[...].astype(F32)
    wide_w[432:864, 0:32] = cw_ref[...].astype(F32)

    def tap(ky, kz, kx):
        at = ((ky * 3 + kz) * 3 + kx) * 16
        return wide_w[at:at + 16, :]

    zero16 = jnp.zeros((16, 128), BF16)
    for z in range(2):
        for ky in range(3):
            base = jnp.zeros((16, 128), F32)
            for kx in range(3):
                for zz in range(2):
                    at = 32 * kx + 16 * zz
                    moved = tap(ky, zz - z + 1, kx)
                    if at:
                        moved = pltpu.roll(moved, at, 1)
                    base = jnp.where((lane >= at) & (lane < at + 16), moved, base)
            for px in range(2):
                block = (pltpu.roll(base, 32, 1) if px else base).astype(BF16)
                for py in range(2):
                    rows = (py * 2 + px) * 32 + z * 16
                    w_fwd[rows:rows + 16, (ky + py) * 128:(ky + py + 1) * 128] = block
    for py in range(2):
        idle = 3 if py == 0 else 0
        for blocks in range(4):
            rows = py * 64 + blocks * 16
            w_fwd[rows:rows + 16, idle * 128:(idle + 1) * 128] = zero16
    spans = {(0, 0): (0,), (0, 1): (1, 2), (0, 2): (), (1, 0): (), (1, 1): (0, 1), (1, 2): (2,)}
    for z in range(2):
        pair = [[tap(ky, 1 - z, kx) + tap(ky, 2 - z, kx) for kx in range(3)] for ky in range(3)]
        for py in range(2):
            for dy in range(3):
                kys = spans[py, dy]
                for px in range(2):
                    rows = (py * 2 + px) * 32 + z * 16
                    block = jnp.zeros((16, 128), F32)
                    for dx in range(3):
                        terms = [pair[ky][kx] for ky in kys for kx in spans[px, dx]]
                        if not terms:
                            continue
                        moved = pltpu.roll(functools.reduce(jnp.add, terms), (32 * dx - 16) % 128, 1)
                        block = jnp.where((lane >= 32 * dx) & (lane < 32 * dx + 32), moved, block)
                    w_fwd[rows:rows + 16, 512 + dy * 128:512 + (dy + 1) * 128] = block.astype(BF16)
    for z in range(2):
        for ky in range(3):
            for wx in range(4):
                for zz in range(2):
                    at = (z * 3 + ky) * 128 + wx * 32 + zz * 16
                    if wx == 3:
                        stack[at:at + 16, :] = zero16
                    else:
                        stack[at:at + 16, :] = tap(2 - ky, 1 + z - zz, 2 - wx).astype(BF16)
    eye = (iota((48, 128), 0) == iota((48, 128), 1)).astype(F32).astype(BF16)
    turned = dot_nt(eye, stack[...])
    w_bwd[...] = jnp.zeros_like(w_bwd)
    act = [jnp.zeros((32, 128), F32) for _ in range(4)]
    for z in range(2):
        for ky in range(3):
            at = (z * 3 + ky) * 128
            base = turned[:, at:at + 128]
            for px in range(2):
                moved = pltpu.roll(base, 32, 1) if px else base
                for py in range(2):
                    rows = (py * 2 + px) * 32 + z * 16
                    w_bwd[rows:rows + 16, (ky + py) * 128:(ky + py + 1) * 128] = moved[0:16].astype(BF16)
                    act[ky + py] = act[ky + py] + moved[16:48]
    for wy in range(4):
        w_bwd[128:160, wy * 128:(wy + 1) * 128] = act[wy].astype(BF16)
    for dy in range(3):
        block = jnp.zeros((16, 128), F32)
        for dx in range(3):
            at = 432 + ((dy * 3 + 1) * 3 + dx) * 16
            stack_c[(dy * 3 + dx) * 16:(dy * 3 + dx + 1) * 16, :] = wide_w[at:at + 16, :].astype(BF16)
            at = 432 + (((2 - dy) * 3 + 1) * 3 + 2 - dx) * 16
            moved = wide_w[at:at + 16, :]
            if dx:
                moved = pltpu.roll(moved, 32 * dx, 1)
            block = jnp.where((lane >= 32 * dx) & (lane < 32 * dx + 32), moved, block)
        w_gp[:, dy * 128:(dy + 1) * 128] = block.astype(BF16)
    w_pre[...] = dot_nt(eye[0:32], stack_c[...]).astype(BF16)


def level_gradients(n_wide, n_narrow, me_y, me_x, ext_ref, left_ref, right_ref, sums_ref,
                    w_bwd, w_pre, fine, cot, pool, act, gpre, keep_gj, sums):
    top, bottom = me_y > 0, me_y < n_wide - 1
    first, last = me_x > 0, me_x < n_narrow - 1

    want = iota((128, 512), 1)
    want = 2 * ((want & 127) - 2) - 1 + (want >> 7)
    spread = (iota((128, 512), 0) == want).astype(F32).astype(BF16)
    side_want = iota((32, 512), 1)
    side_want = 2 * ((side_want & 127) - 2) - 1 + (side_want >> 7)
    side_row = iota((32, 512), 0)
    sides = jnp.concatenate([left_ref[...].astype(F32), right_ref[...].astype(F32)], axis=0)
    turned = jnp.transpose(sides).astype(BF16)
    for k, field in enumerate((fine, cot)):
        west = (side_row >= 4 * k) & (side_row < 4 * k + 4) & (side_want == side_row - 4 * k - 4) & first
        east = (side_row >= 16 + 4 * k) & (side_row < 20 + 4 * k) & (side_want == side_row - 16 - 4 * k + 128) & last
        spread_side = (west | east).astype(F32).astype(BF16)
        for part in range(6):
            at = part * 128
            got = dot(ext_ref[k, at:at + 128, :], spread) + dot(turned[at:at + 128, :], spread_side)
            if part == 0:
                got = jnp.where(top, got, 0.0)
            if part == 5:
                got = jnp.where(bottom, got, 0.0)
            got = got.astype(BF16)
            for y in range(4):
                for wx in range(4):
                    to = (part * 4 + y) * 128 + wx * 32
                    field[to:to + 32, :] = got[y * 32:y * 32 + 32, wx * 128:wx * 128 + 128]

    for r in range(12):
        both = (fine[2 * r * 128 + 32:2 * r * 128 + 96, :].astype(F32)
                + fine[(2 * r + 1) * 128 + 32:(2 * r + 1) * 128 + 96, :].astype(F32))
        mean = (both[0:16] + both[16:32] + both[32:48] + both[48:64]) * 0.125
        pool[r * 48:r * 48 + 16, :] = pltpu.roll(mean, 1, 1).astype(BF16)
        pool[r * 48 + 16:r * 48 + 32, :] = mean.astype(BF16)
        pool[r * 48 + 32:r * 48 + 48, :] = pltpu.roll(mean, 127, 1).astype(BF16)

    lane = iota((32, 128), 1)
    inside = ((lane >= 2) | ((lane == 1) & first)) & ((lane <= 65) | ((lane == 66) & last))
    own = (iota((128, 128), 1) >= 2) & (iota((128, 128), 1) <= 65)
    blank = jnp.zeros((32, 128), BF16)
    for r in range(1, 11):
        pre = dot(w_pre[...], pool[(r - 1) * 48:(r + 2) * 48, :])
        sig = 1.0 / (1.0 + jnp.exp(-pre))
        back = dot(w_bwd[...], cot[(2 * r - 1) * 128:(2 * r + 3) * 128, :])
        grad_act = back[128:160].astype(BF16).astype(F32)
        slope = grad_act * (sig * (1.0 + pre * (1.0 - sig)))
        valid = inside
        if r == 1:
            valid = inside & top
        if r == 10:
            valid = inside & bottom
        for value, to in ((pre * sig, act), (slope, gpre)):
            value = jnp.where(valid, value, 0.0)
            at = (r - 1) * 128
            to[at:at + 32, :] = pltpu.roll(value, 1, 1).astype(BF16)
            to[at + 32:at + 64, :] = value.astype(BF16)
            to[at + 64:at + 96, :] = pltpu.roll(value, 127, 1).astype(BF16)
            to[at + 96:at + 128, :] = blank
        if 2 <= r <= 9:
            keep_gj[(r - 2) * 128:(r - 1) * 128, :] = back[0:128]

    def own_cot(r):
        a, b = 2 * r * 128, (2 * r + 1) * 128
        both = jnp.concatenate([cot[a + 32:a + 96, :], cot[b + 32:b + 96, :]], axis=0)
        return jnp.where(own, both.astype(F32), 0.0).astype(BF16)

    def lanes(parts):
        return jnp.concatenate(parts, axis=1)

    grad = jnp.zeros((128, 512), F32)
    grad_up = jnp.zeros((128, 384), F32)
    grad_c = jnp.zeros((144, 32), F32)
    for r in range(2, 10, 2):
        lhs = lanes([own_cot(r), own_cot(r + 1)])
        grad += dot_nt(lhs, lanes([fine[(2 * q - 1) * 128:(2 * q + 3) * 128, :] for q in (r, r + 1)]))
        grad_up += dot_nt(lhs, lanes([act[(q - 2) * 128:(q + 1) * 128, :] for q in (r, r + 1)]))
        mine = [jnp.where(own[0:32], gpre[(q - 1) * 128 + 32:(q - 1) * 128 + 64, :].astype(F32), 0.0).astype(BF16)
                for q in (r, r + 1)]
        grad_c += dot_nt(lanes([pool[(q - 1) * 48:(q + 2) * 48, :] for q in (r, r + 1)]), lanes(mine))
    dys = ((0, 1, 1), (1, 1, 2))
    taps = [jnp.concatenate([grad_c[t * 16:t * 16 + 16], jnp.zeros((16, 96), F32)], axis=1) for t in range(9)]
    none = jnp.zeros((16, 128), F32)
    for block in range(6):
        if block < 3:
            ky = block
            total = sum(grad[py * 64:py * 64 + 32, (ky + py) * 128:(ky + py + 1) * 128] for py in range(2))
            odd = sum(grad[py * 64 + 32:py * 64 + 64, (ky + py) * 128:(ky + py + 1) * 128] for py in range(2))
            total = total + pltpu.roll(odd, 96, 1)
        else:
            ky = block - 3
            even, odd = (sum(grad_up[py * 64 + px * 32:py * 64 + px * 32 + 32, dys[py][ky] * 128:(dys[py][ky] + 1) * 128]
                             for py in range(2)) for px in range(2))
            total = jnp.where(lane < 64, even, pltpu.roll(even, 32, 1)) + jnp.where(lane < 32, pltpu.roll(odd, 96, 1), odd)
        extra = jnp.concatenate([taps[t] if t < 9 else none for t in (2 * block, 2 * block + 1)], axis=0)
        sums[block * 32:block * 32 + 32, :] = jnp.where(lane < 96, total, pltpu.roll(extra, 96, 1))
    count, depth = sums_ref.shape[0], sums_ref.shape[1]
    for j in range(count):
        sums_ref[j] = sums[j * depth:(j + 1) * depth, :]


def level_outputs(out_ref, gf_ref, w_fwd, w_gp, fine, act, gpre, keep_gj, flat, turn):
    joiner = iota((256, 128), 0)
    joiner = (2 * ((joiner & 127) - 2) + (joiner >> 7) == iota((256, 128), 1)).astype(F32).astype(BF16)

    def place(values, r):
        values = values.astype(BF16)
        for py in range(2):
            at = (2 * (r - 2) + py) * 32
            flat[at:at + 32, 0:128] = values[py * 64:py * 64 + 32]
            flat[at:at + 32, 128:256] = values[py * 64 + 32:py * 64 + 64]

    def finish(to):
        for part in range(4):
            joined = dot(flat[part * 128:part * 128 + 128, :], joiner)
            for j in range(8):
                turn[pl.ds(part * 8 + j, 16, stride=32), :] = joined[j * 16:j * 16 + 16]
        to[...] = turn[...].astype(BF16)

    for r in range(2, 10):
        got = dot(w_fwd[:, 0:512], fine[(2 * r - 1) * 128:(2 * r + 3) * 128, :])
        got += dot(w_fwd[:, 512:896], act[(r - 2) * 128:(r + 1) * 128, :])
        place(got, r)
    finish(out_ref)
    for r in range(2, 10):
        low = dot(w_gp[...], gpre[(r - 2) * 128:(r + 1) * 128, :]).astype(BF16).astype(F32) * 0.125
        place(keep_gj[(r - 2) * 128:(r - 1) * 128, :] + jnp.concatenate([low] * 8, axis=0), r)
    finish(gf_ref)


def main_kernel(n_wide, n_narrow, f_hbm, c_hbm, fw_hbm, cw_hbm, out_hbm, gf_hbm, total_ref,
                f_ref, c_ref, fw_ref, cw_ref, in_sem,
                wide32, go_left, go_right, ext, left, right, halo_send, halo_recv,
                wide_w, stack, w_fwd, w_bwd, stack_c, w_pre, w_gp,
                fine, cot, pool, act, gpre, keep_gj, flat, turn, sums,
                out_v, gf_v, out_sem, mine, got1, part, got2, fin, send1, recv1, send2, recv2, send3, recv3):
    g1, g2 = n_wide // OUTER, n_narrow * OUTER
    depth = ROWS // g1
    len_y, len_z, len_x = g1 // 2, 2 * OUTER, n_narrow // 2
    me_y, me_x = lax.axis_index("wide"), lax.axis_index("narrow")
    me1 = lax.rem(me_y, g1)
    run_z = lax.div(me_y, g1)
    at_y, at_core = lax.div(me1, 2), lax.rem(me1, 2)
    at_z, at_x = lax.rem(me_x, 2) * OUTER + run_z, lax.div(me_x, 2)
    me2 = at_x * len_z + at_z

    def far_first(sizes):
        steps = [(a, b) for a in range(sizes[0]) for b in range(sizes[1]) if a or b]
        return sorted(steps, key=lambda s: -sum(min(k, n - k) for k, n in zip(s, sizes)))

    first, second = [], []
    for dy, dcore in far_first((len_y, 2)):
        k = lax.rem(at_y + dy, len_y) * 2 + lax.rem(at_core + dcore, 2)
        first.append((k, (run_z * g1 + k, me_x)))
    for dz, dx in far_first((len_z, len_x)):
        z, x = lax.rem(at_z + dz, len_z), lax.rem(at_x + dx, len_x)
        second.append((x * len_z + z, (lax.rem(z, OUTER) * g1 + me1, x * 2 + lax.div(z, OUTER))))

    barrier = pltpu.get_barrier_semaphore()
    near = neighbours(n_wide, n_narrow, me_y, me_x)
    for device in near + [device for _, device in second + first]:
        pl.semaphore_signal(barrier, inc=1, device_id=device, device_id_type=MESH)
    reads = [pltpu.make_async_copy(src, dst, in_sem.at[j]) for j, (src, dst) in enumerate(
        ((f_hbm, f_ref), (c_hbm, c_ref), (fw_hbm, fw_ref), (cw_hbm, cw_ref)))]
    for read in reads:
        read.start()
    for read in reads[:2]:
        read.wait()
    pack_own(f_ref, c_ref, ext, wide32, go_left, go_right)
    for read in reads[2:]:
        read.wait()
    prepare_weights(fw_ref, cw_ref, wide_w, stack, w_fwd, w_bwd, stack_c, w_pre, w_gp)
    pl.semaphore_wait(barrier, 8 + g1 + g2 - 2)
    halo = halo_copies(near, ext, left, right, go_left, go_right, halo_send, halo_recv)
    for j in (4, 5, 6, 7, 2, 3, 0, 1):
        halo[j].start()
    for copy in halo:
        copy.wait_recv()
    level_gradients(n_wide, n_narrow, me_y, me_x, ext, left, right, mine,
                    w_bwd, w_pre, fine, cot, pool, act, gpre, keep_gj, sums)

    def send_all(group, source, slot, sends, receives):
        for j, (k, device) in enumerate(group):
            pltpu.make_async_remote_copy(
                src_ref=source(k), dst_ref=slot(j), send_sem=sends, recv_sem=receives,
                device_id=device, device_id_type=MESH).start()

    def all_of(ref, sends, receives):
        return pltpu.make_async_remote_copy(
            src_ref=ref, dst_ref=ref, send_sem=sends, recv_sem=receives,
            device_id=near[0], device_id_type=MESH)

    one = all_of(got1, send1, recv1)
    two = all_of(got2.at[pl.ds(0, g2 - 1)], send2, recv2)
    three = all_of(fin.at[pl.ds(0, g1 - 1)], send3, recv3)
    send_all(first, lambda k: mine.at[k], lambda j: got1.at[j], send1, recv1)
    level_outputs(out_v, gf_v, w_fwd, w_gp, fine, act, gpre, keep_gj, flat, turn)
    writes = [pltpu.make_async_copy(out_v, out_hbm, out_sem.at[0]), pltpu.make_async_copy(gf_v, gf_hbm, out_sem.at[1])]
    for write in writes:
        write.start()
    one.wait_recv()
    total = mine[me1]
    for j in range(g1 - 1):
        total += got1[j]
    part[...] = total
    send_all(second, lambda k: part, lambda j: got2.at[me2], send2, recv2)
    got2[me2] = total
    for copy in halo:
        copy.wait_send()
    one.wait_send()
    for write in writes:
        write.wait()
    two.wait_recv()
    total = got2[0]
    for k in range(1, g2):
        total += got2[k]
    fin[me1] = total
    send_all(first, lambda k: fin.at[me1], lambda j: fin.at[me1], send3, recv3)
    two.wait_send()
    three.wait_recv()
    for j in range(g1):
        total_ref[j * depth:(j + 1) * depth, :] = fin[j]
    three.wait_send()


def finish_kernel(scale_fine, scale_coarse, turn, out_in, gf_in, gfine_ref, gcoarse_ref, out_ref, gf_ref, sem):
    copies = [pltpu.make_async_copy(out_in, out_ref, sem.at[0]), pltpu.make_async_copy(gf_in, gf_ref, sem.at[1])]
    for copy in copies:
        copy.start()
    lane = iota((16, 128), 1)
    for ky in range(3):
        flow = [turn[ky * 32 + z * 16:ky * 32 + z * 16 + 16, :] for z in range(2)]
        rise = [turn[96 + ky * 32 + z * 16:96 + ky * 32 + z * 16 + 16, :] for z in range(2)]
        ups = (rise[1], rise[0] + rise[1], rise[0])
        for kx in range(3):
            near0 = [pltpu.roll(flow[z], (-32 * kx) % 128, 1) if kx else flow[z] for z in range(2)]
            near1 = [pltpu.roll(flow[z], (-32 * kx - 16) % 128, 1) for z in range(2)]
            own = (near0[1], near0[0] + near1[1], near1[0])
            for kz in range(3):
                whole = jnp.where(lane < 16, own[kz], pltpu.roll(ups[kz], (16 - 32 * kx) % 128, 1))
                at = ((ky * 3 + kz) * 3 + kx) * 16
                gfine_ref[at:at + 16, :] = (whole * scale_fine)[:, 0:48]
                if kz == 1:
                    t = ky * 3 + kx
                    row = (t // 2) * 32 + (t % 2) * 16
                    coarse = pltpu.roll(turn[row:row + 16, :], 32, 1)[:, 0:32] * scale_coarse
                    gcoarse_ref[at:at + 16, :] = coarse
                else:
                    gcoarse_ref[at:at + 16, :] = jnp.zeros((16, 32), F32)
    for copy in copies:
        copy.wait()


def shards(n_wide, n_narrow, features, cotangent, coarse_weight, fine_weight):
    inside = pl.BlockSpec(memory_space=VMEM)
    shape = jax.ShapeDtypeStruct
    g1, g2 = n_wide // OUTER, n_narrow * OUTER
    depth = ROWS // g1
    cells = n_wide * 16 * 2 * n_narrow * 128
    fw = jnp.transpose(fine_weight, (2, 3, 4, 0, 1)).reshape(432, 48)
    cw = jnp.transpose(coarse_weight, (2, 3, 4, 1, 0)).reshape(432, 32)
    dma = pltpu.SemaphoreType.DMA
    large = pl.BlockSpec(memory_space=pl.ANY)
    output, grad_features, sums = pl.pallas_call(
        functools.partial(main_kernel, n_wide, n_narrow),
        out_shape=(shape((512, 128), BF16), shape((512, 128), BF16), shape((ROWS, 128), F32)),
        in_specs=[large] * 4,
        out_specs=(large, large, inside),
        scratch_shapes=[
            VMEM((512, 128), BF16), VMEM((512, 128), BF16), VMEM((432, 48), BF16), VMEM((432, 32), BF16), dma((4,)),
            VMEM((2, 512, 128), F32), VMEM((16, 512), BF16), VMEM((16, 512), BF16),
            VMEM((2, 768, 128), BF16), VMEM((16, 768), BF16), VMEM((16, 768), BF16), dma((8,)), dma((8,)),
            VMEM((864, 128), F32), VMEM((768, 128), BF16), VMEM((128, 896), BF16), VMEM((160, 512), BF16),
            VMEM((144, 128), BF16), VMEM((32, 144), BF16), VMEM((16, 384), BF16),
            VMEM((3072, 128), BF16), VMEM((3072, 128), BF16), VMEM((576, 128), BF16),
            VMEM((1280, 128), BF16), VMEM((1280, 128), BF16), VMEM((1024, 128), F32),
            VMEM((512, 256), BF16), VMEM((512, 128), F32), VMEM((ROWS, 128), F32),
            VMEM((512, 128), BF16), VMEM((512, 128), BF16), dma((2,)),
            VMEM((g1, depth, 128), F32), VMEM((g1 - 1, depth, 128), F32), VMEM((depth, 128), F32),
            VMEM((g2, depth, 128), F32), VMEM((g1, depth, 128), F32),
            dma, dma, dma, dma, dma, dma,
        ],
        compiler_params=pltpu.CompilerParams(
            collective_id=0, has_side_effects=True, vmem_limit_bytes=56 * 1024 * 1024),
        name="levels",
    )(features.reshape(512, 128), cotangent.reshape(512, 128), fw, cw)
    gfine, gcoarse, output, grad_features = pl.pallas_call(
        functools.partial(finish_kernel, 1.0 / math.sqrt(cells), 1.0 / math.sqrt(cells // 8)),
        out_shape=(shape((432, 48), F32), shape((432, 32), F32), shape((512, 128), BF16), shape((512, 128), BF16)),
        in_specs=[inside] * 3,
        out_specs=(inside, inside, large, large),
        scratch_shapes=[dma((2,))],
        name="finish",
    )(sums, output, grad_features)
    return (
        output.reshape(16, 16, 2, 128),
        grad_features.reshape(16, 16, 2, 128),
        jnp.transpose(gfine.reshape(3, 3, 3, 16, 48), (3, 4, 0, 1, 2)),
        jnp.transpose(gcoarse.reshape(3, 3, 3, 16, 32), (4, 3, 0, 1, 2)),
    )


def solution(mesh):
    placed = P(None, "wide", None, "narrow")
    return jax.shard_map(
        functools.partial(shards, mesh.shape["wide"], mesh.shape["narrow"]),
        mesh=mesh,
        in_specs=(placed, placed, P(), P()),
        out_specs=(placed, placed, P(), P()),
        check_vma=False,
    )
```

```python
import functools
import math

import jax
import jax.numpy as jnp
from jax import lax
from jax.experimental import pallas as pl
from jax.experimental.pallas import tpu as pltpu
from jax.sharding import PartitionSpec as P

F32, BF16 = jnp.float32, jnp.bfloat16
MESH = pl.DeviceIdType.MESH
VMEM = pltpu.VMEM
OUTER = 4
ROWS = 192


def dot(a, b):
    return lax.dot_general(a, b, (((1,), (0,)), ((), ())), preferred_element_type=F32)


def dot_nt(a, b):
    return lax.dot_general(a, b, (((1,), (1,)), ((), ())), preferred_element_type=F32)


def iota(shape, axis):
    return lax.broadcasted_iota(jnp.int32, shape, axis)


def neighbours(n_wide, n_narrow, me_y, me_x):
    up, down = lax.rem(me_y + n_wide - 1, n_wide), lax.rem(me_y + 1, n_wide)
    west, east = lax.rem(me_x + n_narrow - 1, n_narrow), lax.rem(me_x + 1, n_narrow)
    return [(up, me_x), (down, me_x), (me_y, west), (me_y, east),
            (up, west), (up, east), (down, west), (down, east)]


def pack_own(f_ref, c_ref, ext_ref, wide32, go_left, go_right):
    for k, ref in enumerate((f_ref, c_ref)):
        wide32[k] = ref[...].astype(F32)
        for j in range(32):
            part = wide32[k, pl.ds(j, 16, stride=32), :]
            ext_ref[k, 128 + 16 * j:144 + 16 * j, :] = part.astype(BF16)
    row, col = iota((16, 128), 0), iota((16, 128), 1)
    for start, buf in ((0, go_left), (124, go_right)):
        total = jnp.zeros((16, 512), F32)
        for k in range(2):
            pick = (row >= 4 * k) & (row < 4 * k + 4) & (col == start + row - 4 * k)
            total += dot_nt(pick.astype(F32).astype(BF16), ext_ref[k, 128:640, :])
        buf[...] = total.astype(BF16)


def halo_copies(near, ext_ref, left_ref, right_ref, go_left, go_right, send, recv):
    plan = [
        (ext_ref.at[:, pl.ds(128, 128), :], ext_ref.at[:, pl.ds(640, 128), :]),
        (ext_ref.at[:, pl.ds(512, 128), :], ext_ref.at[:, pl.ds(0, 128), :]),
        (go_left, right_ref.at[:, pl.ds(128, 512)]),
        (go_right, left_ref.at[:, pl.ds(128, 512)]),
        (go_left.at[:, pl.ds(0, 128)], right_ref.at[:, pl.ds(640, 128)]),
        (go_right.at[:, pl.ds(0, 128)], left_ref.at[:, pl.ds(640, 128)]),
        (go_left.at[:, pl.ds(384, 128)], right_ref.at[:, pl.ds(0, 128)]),
        (go_right.at[:, pl.ds(384, 128)], left_ref.at[:, pl.ds(0, 128)]),
    ]
    return [
        pltpu.make_async_remote_copy(
            src_ref=src, dst_ref=dst, send_sem=send.at[j], recv_sem=recv.at[j],
            device_id=near[j], device_id_type=MESH)
        for j, (src, dst) in enumerate(plan)
    ]


def prepare_weights(fw_ref, cw_ref, wide_w, stack, w_fwd, w_bwd, stack_c, w_pre, w_gp):
    lane = iota((16, 128), 1)
    wide_w[...] = jnp.zeros_like(wide_w)
    wide_w[0:432, 0:48] = fw_ref[...].astype(F32)
    wide_w[432:864, 0:32] = cw_ref[...].astype(F32)

    def tap(ky, kz, kx):
        at = ((ky * 3 + kz) * 3 + kx) * 16
        return wide_w[at:at + 16, :]

    zero16 = jnp.zeros((16, 128), BF16)
    for z in range(2):
        for ky in range(3):
            base = jnp.zeros((16, 128), F32)
            for kx in range(3):
                for zz in range(2):
                    at = 32 * kx + 16 * zz
                    moved = tap(ky, zz - z + 1, kx)
                    if at:
                        moved = pltpu.roll(moved, at, 1)
                    base = jnp.where((lane >= at) & (lane < at + 16), moved, base)
            for px in range(2):
                block = (pltpu.roll(base, 32, 1) if px else base).astype(BF16)
                for py in range(2):
                    rows = (py * 2 + px) * 32 + z * 16
                    w_fwd[rows:rows + 16, (ky + py) * 128:(ky + py + 1) * 128] = block
    for py in range(2):
        idle = 3 if py == 0 else 0
        for blocks in range(4):
            rows = py * 64 + blocks * 16
            w_fwd[rows:rows + 16, idle * 128:(idle + 1) * 128] = zero16
    spans = {(0, 0): (0,), (0, 1): (1, 2), (0, 2): (), (1, 0): (), (1, 1): (0, 1), (1, 2): (2,)}
    for z in range(2):
        pair = [[tap(ky, 1 - z, kx) + tap(ky, 2 - z, kx) for kx in range(3)] for ky in range(3)]
        for py in range(2):
            for dy in range(3):
                kys = spans[py, dy]
                for px in range(2):
                    rows = (py * 2 + px) * 32 + z * 16
                    block = jnp.zeros((16, 128), F32)
                    for dx in range(3):
                        terms = [pair[ky][kx] for ky in kys for kx in spans[px, dx]]
                        if not terms:
                            continue
                        moved = pltpu.roll(functools.reduce(jnp.add, terms), (32 * dx - 16) % 128, 1)
                        block = jnp.where((lane >= 32 * dx) & (lane < 32 * dx + 32), moved, block)
                    w_fwd[rows:rows + 16, 512 + dy * 128:512 + (dy + 1) * 128] = block.astype(BF16)
    for z in range(2):
        for ky in range(3):
            for wx in range(4):
                for zz in range(2):
                    at = (z * 3 + ky) * 128 + wx * 32 + zz * 16
                    if wx == 3:
                        stack[at:at + 16, :] = zero16
                    else:
                        stack[at:at + 16, :] = tap(2 - ky, 1 + z - zz, 2 - wx).astype(BF16)
    eye = (iota((48, 128), 0) == iota((48, 128), 1)).astype(F32).astype(BF16)
    turned = dot_nt(eye, stack[...])
    w_bwd[...] = jnp.zeros_like(w_bwd)
    act = [jnp.zeros((32, 128), F32) for _ in range(4)]
    for z in range(2):
        for ky in range(3):
            at = (z * 3 + ky) * 128
            base = turned[:, at:at + 128]
            for px in range(2):
                moved = pltpu.roll(base, 32, 1) if px else base
                for py in range(2):
                    rows = (py * 2 + px) * 32 + z * 16
                    w_bwd[rows:rows + 16, (ky + py) * 128:(ky + py + 1) * 128] = moved[0:16].astype(BF16)
                    act[ky + py] = act[ky + py] + moved[16:48]
    for wy in range(4):
        w_bwd[128:160, wy * 128:(wy + 1) * 128] = act[wy].astype(BF16)
    for dy in range(3):
        block = jnp.zeros((16, 128), F32)
        for dx in range(3):
            at = 432 + ((dy * 3 + 1) * 3 + dx) * 16
            stack_c[(dy * 3 + dx) * 16:(dy * 3 + dx + 1) * 16, :] = wide_w[at:at + 16, :].astype(BF16)
            at = 432 + (((2 - dy) * 3 + 1) * 3 + 2 - dx) * 16
            moved = wide_w[at:at + 16, :]
            if dx:
                moved = pltpu.roll(moved, 32 * dx, 1)
            block = jnp.where((lane >= 32 * dx) & (lane < 32 * dx + 32), moved, block)
        w_gp[:, dy * 128:(dy + 1) * 128] = block.astype(BF16)
    w_pre[...] = dot_nt(eye[0:32], stack_c[...]).astype(BF16)


def level_gradients(n_wide, n_narrow, me_y, me_x, ext_ref, left_ref, right_ref, sums_ref,
                    w_bwd, w_pre, fine, cot, pool, act, gpre, keep_gj, sums):
    top, bottom = me_y > 0, me_y < n_wide - 1
    first, last = me_x > 0, me_x < n_narrow - 1

    want = iota((128, 512), 1)
    want = 2 * ((want & 127) - 2) - 1 + (want >> 7)
    spread = (iota((128, 512), 0) == want).astype(F32).astype(BF16)
    side_want = iota((32, 512), 1)
    side_want = 2 * ((side_want & 127) - 2) - 1 + (side_want >> 7)
    side_row = iota((32, 512), 0)
    sides = jnp.concatenate([left_ref[...].astype(F32), right_ref[...].astype(F32)], axis=0)
    turned = jnp.transpose(sides).astype(BF16)
    for k, field in enumerate((fine, cot)):
        west = (side_row >= 4 * k) & (side_row < 4 * k + 4) & (side_want == side_row - 4 * k - 4) & first
        east = (side_row >= 16 + 4 * k) & (side_row < 20 + 4 * k) & (side_want == side_row - 16 - 4 * k + 128) & last
        both = jnp.concatenate([spread, (west | east).astype(F32).astype(BF16)], axis=0)
        for part in range(6):
            at = part * 128
            got = dot(jnp.concatenate([ext_ref[k, at:at + 128, :], turned[at:at + 128, :]], axis=1), both)
            if part == 0:
                got = jnp.where(top, got, 0.0)
            if part == 5:
                got = jnp.where(bottom, got, 0.0)
            got = got.astype(BF16)
            for y in range(4):
                for wx in range(4):
                    to = (part * 4 + y) * 128 + wx * 32
                    field[to:to + 32, :] = got[y * 32:y * 32 + 32, wx * 128:wx * 128 + 128]

    for r in range(12):
        both = (fine[2 * r * 128 + 32:2 * r * 128 + 96, :].astype(F32)
                + fine[(2 * r + 1) * 128 + 32:(2 * r + 1) * 128 + 96, :].astype(F32))
        mean = (both[0:16] + both[16:32] + both[32:48] + both[48:64]) * 0.125
        pool[r * 48:r * 48 + 16, :] = pltpu.roll(mean, 1, 1).astype(BF16)
        pool[r * 48 + 16:r * 48 + 32, :] = mean.astype(BF16)
        pool[r * 48 + 32:r * 48 + 48, :] = pltpu.roll(mean, 127, 1).astype(BF16)

    lane = iota((32, 128), 1)
    inside = ((lane >= 2) | ((lane == 1) & first)) & ((lane <= 65) | ((lane == 66) & last))
    own = (iota((128, 128), 1) >= 2) & (iota((128, 128), 1) <= 65)
    blank = jnp.zeros((32, 128), BF16)
    for r in range(1, 11):
        pre = dot(w_pre[...], pool[(r - 1) * 48:(r + 2) * 48, :])
        sig = 1.0 / (1.0 + jnp.exp(-pre))
        back = dot(w_bwd[...], cot[(2 * r - 1) * 128:(2 * r + 3) * 128, :])
        grad_act = back[128:160].astype(BF16).astype(F32)
        slope = grad_act * (sig * (1.0 + pre * (1.0 - sig)))
        valid = inside
        if r == 1:
            valid = inside & top
        if r == 10:
            valid = inside & bottom
        for value, to in ((pre * sig, act), (slope, gpre)):
            value = jnp.where(valid, value, 0.0)
            at = (r - 1) * 128
            to[at:at + 32, :] = pltpu.roll(value, 1, 1).astype(BF16)
            to[at + 32:at + 64, :] = value.astype(BF16)
            to[at + 64:at + 96, :] = pltpu.roll(value, 127, 1).astype(BF16)
            to[at + 96:at + 128, :] = blank
        if 2 <= r <= 9:
            keep_gj[(r - 2) * 128:(r - 1) * 128, :] = back[0:128]

    def own_cot(r):
        a, b = 2 * r * 128, (2 * r + 1) * 128
        both = jnp.concatenate([cot[a + 32:a + 96, :], cot[b + 32:b + 96, :]], axis=0)
        return jnp.where(own, both.astype(F32), 0.0).astype(BF16)

    def lanes(parts):
        return jnp.concatenate(parts, axis=1)

    rows = range(2, 10)
    lhs = lanes([own_cot(r) for r in rows])
    grad = dot_nt(lhs, lanes([fine[(2 * r - 1) * 128:(2 * r + 3) * 128, :] for r in rows]))
    grad_up = dot_nt(lhs, lanes([act[(r - 2) * 128:(r + 1) * 128, :] for r in rows]))
    grad_c = dot_nt(
        lanes([pool[(r - 1) * 48:(r + 2) * 48, :] for r in rows]),
        lanes([jnp.where(own[0:32], gpre[(r - 1) * 128 + 32:(r - 1) * 128 + 64, :].astype(F32), 0.0).astype(BF16)
               for r in rows]))
    dys = ((0, 1, 1), (1, 1, 2))
    taps = [jnp.concatenate([grad_c[t * 16:t * 16 + 16], jnp.zeros((16, 96), F32)], axis=1) for t in range(9)]
    none = jnp.zeros((16, 128), F32)
    for block in range(6):
        if block < 3:
            ky = block
            total = sum(grad[py * 64:py * 64 + 32, (ky + py) * 128:(ky + py + 1) * 128] for py in range(2))
            odd = sum(grad[py * 64 + 32:py * 64 + 64, (ky + py) * 128:(ky + py + 1) * 128] for py in range(2))
            total = total + pltpu.roll(odd, 96, 1)
        else:
            ky = block - 3
            even, odd = (sum(grad_up[py * 64 + px * 32:py * 64 + px * 32 + 32, dys[py][ky] * 128:(dys[py][ky] + 1) * 128]
                             for py in range(2)) for px in range(2))
            total = jnp.where(lane < 64, even, pltpu.roll(even, 32, 1)) + jnp.where(lane < 32, pltpu.roll(odd, 96, 1), odd)
        extra = jnp.concatenate([taps[t] if t < 9 else none for t in (2 * block, 2 * block + 1)], axis=0)
        sums[block * 32:block * 32 + 32, :] = jnp.where(lane < 96, total, pltpu.roll(extra, 96, 1))
    count, depth = sums_ref.shape[0], sums_ref.shape[1]
    for j in range(count):
        sums_ref[j] = sums[j * depth:(j + 1) * depth, :].astype(sums_ref.dtype)


def level_outputs(out_ref, gf_ref, w_fwd, w_gp, fine, act, gpre, keep_gj, flat, turn):
    joiner = iota((256, 128), 0)
    joiner = (2 * ((joiner & 127) - 2) + (joiner >> 7) == iota((256, 128), 1)).astype(F32).astype(BF16)

    def place(values, r):
        values = values.astype(BF16)
        for py in range(2):
            at = (2 * (r - 2) + py) * 32
            flat[at:at + 32, 0:128] = values[py * 64:py * 64 + 32]
            flat[at:at + 32, 128:256] = values[py * 64 + 32:py * 64 + 64]

    def finish(to):
        for part in range(4):
            joined = dot(flat[part * 128:part * 128 + 128, :], joiner)
            for j in range(8):
                turn[pl.ds(part * 8 + j, 16, stride=32), :] = joined[j * 16:j * 16 + 16]
        to[...] = turn[...].astype(BF16)

    for r in range(2, 10):
        got = dot(w_fwd[:, 0:512], fine[(2 * r - 1) * 128:(2 * r + 3) * 128, :])
        got += dot(w_fwd[:, 512:896], act[(r - 2) * 128:(r + 1) * 128, :])
        place(got, r)
    finish(out_ref)
    for r in range(2, 10):
        low = dot(w_gp[...], gpre[(r - 2) * 128:(r + 1) * 128, :]).astype(BF16).astype(F32) * 0.125
        place(keep_gj[(r - 2) * 128:(r - 1) * 128, :] + jnp.concatenate([low] * 8, axis=0), r)
    finish(gf_ref)


def main_kernel(n_wide, n_narrow, f_hbm, c_hbm, fw_hbm, cw_hbm, out_hbm, gf_hbm, total_ref,
                f_ref, c_ref, fw_ref, cw_ref, in_sem,
                wide32, go_left, go_right, ext, left, right, halo_send, halo_recv,
                wide_w, stack, w_fwd, w_bwd, stack_c, w_pre, w_gp,
                fine, cot, pool, act, gpre, keep_gj, flat, turn, sums,
                out_v, gf_v, out_sem, mine, got1, part, got2, fin, send1, recv1, send2, recv2, send3, recv3):
    g1, g2 = n_wide // OUTER, n_narrow * OUTER
    depth = ROWS // g1
    len_y, len_z, len_x = g1 // 2, 2 * OUTER, n_narrow // 2
    me_y, me_x = lax.axis_index("wide"), lax.axis_index("narrow")
    me1 = lax.rem(me_y, g1)
    run_z = lax.div(me_y, g1)
    at_y, at_core = lax.div(me1, 2), lax.rem(me1, 2)
    at_z, at_x = lax.rem(me_x, 2) * OUTER + run_z, lax.div(me_x, 2)
    me2 = at_x * len_z + at_z

    def far_first(sizes):
        steps = [(a, b) for a in range(sizes[0]) for b in range(sizes[1]) if a or b]
        return sorted(steps, key=lambda s: -sum(min(k, n - k) for k, n in zip(s, sizes)))

    first, second = [], []
    for dy, dcore in far_first((len_y, 2)):
        k = lax.rem(at_y + dy, len_y) * 2 + lax.rem(at_core + dcore, 2)
        first.append((k, (run_z * g1 + k, me_x)))
    for dz, dx in far_first((len_z, len_x)):
        z, x = lax.rem(at_z + dz, len_z), lax.rem(at_x + dx, len_x)
        second.append((x * len_z + z, (lax.rem(z, OUTER) * g1 + me1, x * 2 + lax.div(z, OUTER))))

    barrier = pltpu.get_barrier_semaphore()
    near = neighbours(n_wide, n_narrow, me_y, me_x)
    for device in near + [device for _, device in second + first]:
        pl.semaphore_signal(barrier, inc=1, device_id=device, device_id_type=MESH)
    reads = [pltpu.make_async_copy(src, dst, in_sem.at[j]) for j, (src, dst) in enumerate(
        ((f_hbm, f_ref), (c_hbm, c_ref), (fw_hbm, fw_ref), (cw_hbm, cw_ref)))]
    for read in reads:
        read.start()
    for read in reads[:2]:
        read.wait()
    pack_own(f_ref, c_ref, ext, wide32, go_left, go_right)
    pl.semaphore_wait(barrier, 8 + g1 + g2 - 2)
    halo = halo_copies(near, ext, left, right, go_left, go_right, halo_send, halo_recv)
    for j in (4, 5, 6, 7, 2, 3, 0, 1):
        halo[j].start()
    for read in reads[2:]:
        read.wait()
    prepare_weights(fw_ref, cw_ref, wide_w, stack, w_fwd, w_bwd, stack_c, w_pre, w_gp)
    for copy in halo:
        copy.wait_recv()
    level_gradients(n_wide, n_narrow, me_y, me_x, ext, left, right, mine,
                    w_bwd, w_pre, fine, cot, pool, act, gpre, keep_gj, sums)

    def send_all(group, source, slot, sends, receives):
        for j, (k, device) in enumerate(group):
            pltpu.make_async_remote_copy(
                src_ref=source(k), dst_ref=slot(j), send_sem=sends, recv_sem=receives,
                device_id=device, device_id_type=MESH).start()

    def all_of(ref, sends, receives):
        return pltpu.make_async_remote_copy(
            src_ref=ref, dst_ref=ref, send_sem=sends, recv_sem=receives,
            device_id=near[0], device_id_type=MESH)

    one = all_of(got1, send1, recv1)
    two = all_of(got2.at[pl.ds(0, g2 - 1)], send2, recv2)
    three = all_of(fin.at[pl.ds(0, g1 - 1)], send3, recv3)
    send_all(first, lambda k: mine.at[k], lambda j: got1.at[j], send1, recv1)
    level_outputs(out_v, gf_v, w_fwd, w_gp, fine, act, gpre, keep_gj, flat, turn)
    writes = [pltpu.make_async_copy(out_v, out_hbm, out_sem.at[0]), pltpu.make_async_copy(gf_v, gf_hbm, out_sem.at[1])]
    for write in writes:
        write.start()
    one.wait_recv()
    total = mine[me1].astype(F32)
    for j in range(g1 - 1):
        total += got1[j].astype(F32)
    part[...] = total.astype(part.dtype)
    send_all(second, lambda k: part, lambda j: got2.at[me2], send2, recv2)
    got2[me2] = part[...]
    for copy in halo:
        copy.wait_send()
    one.wait_send()
    for write in writes:
        write.wait()
    two.wait_recv()
    total = got2[0].astype(F32)
    for k in range(1, g2):
        total += got2[k].astype(F32)
    fin[me1] = total.astype(fin.dtype)
    send_all(first, lambda k: fin.at[me1], lambda j: fin.at[me1], send3, recv3)
    two.wait_send()
    three.wait_recv()
    for j in range(g1):
        total_ref[j * depth:(j + 1) * depth, :] = fin[j].astype(F32)
    three.wait_send()


def finish_kernel(scale_fine, scale_coarse, turn_in, out_in, gf_in, gfine_out, gcoarse_out, out_ref, gf_ref,
                  turn, out_v, gf_v, gfine_ref, gcoarse_ref, sem):
    def copy(src, dst, j):
        return pltpu.make_async_copy(src, dst, sem.at[j])

    reads = [copy(turn_in, turn, 0), copy(out_in, out_v, 1), copy(gf_in, gf_v, 2)]
    writes = [copy(out_v, out_ref, 3), copy(gf_v, gf_ref, 4)]
    for read in reads:
        read.start()
    reads[0].wait()
    lane = iota((16, 128), 1)
    for ky in range(3):
        if ky:
            reads[ky].wait()
            writes[ky - 1].start()
        flow = [turn[ky * 32 + z * 16:ky * 32 + z * 16 + 16, :] for z in range(2)]
        rise = [turn[96 + ky * 32 + z * 16:96 + ky * 32 + z * 16 + 16, :] for z in range(2)]
        ups = (rise[1], rise[0] + rise[1], rise[0])
        for kx in range(3):
            near0 = [pltpu.roll(flow[z], (-32 * kx) % 128, 1) if kx else flow[z] for z in range(2)]
            near1 = [pltpu.roll(flow[z], (-32 * kx - 16) % 128, 1) for z in range(2)]
            own = (near0[1], near0[0] + near1[1], near1[0])
            for kz in range(3):
                whole = jnp.where(lane < 16, own[kz], pltpu.roll(ups[kz], (16 - 32 * kx) % 128, 1))
                at = ((ky * 3 + kz) * 3 + kx) * 16
                gfine_ref[at:at + 16, :] = (whole * scale_fine)[:, 0:48]
                if kz == 1:
                    t = ky * 3 + kx
                    row = (t // 2) * 32 + (t % 2) * 16
                    coarse = pltpu.roll(turn[row:row + 16, :], 32, 1)[:, 0:32] * scale_coarse
                    gcoarse_ref[at:at + 16, :] = coarse
                else:
                    gcoarse_ref[at:at + 16, :] = jnp.zeros((16, 32), F32)
        for j, (src, dst) in enumerate(((gfine_ref, gfine_out), (gcoarse_ref, gcoarse_out))):
            rows = pl.ds(ky * 144, 144)
            writes.append(copy(src.at[rows, :], dst.at[rows, :], 5 + 2 * ky + j))
            writes[-1].start()
    for write in writes:
        write.wait()


def shards(n_wide, n_narrow, features, cotangent, coarse_weight, fine_weight):
    inside = pl.BlockSpec(memory_space=VMEM)
    shape = jax.ShapeDtypeStruct
    g1, g2 = n_wide // OUTER, n_narrow * OUTER
    depth = ROWS // g1
    cells = n_wide * 16 * 2 * n_narrow * 128
    fw = jnp.transpose(fine_weight, (2, 3, 4, 0, 1)).reshape(432, 48)
    cw = jnp.transpose(coarse_weight, (2, 3, 4, 1, 0)).reshape(432, 32)
    dma = pltpu.SemaphoreType.DMA
    large = pl.BlockSpec(memory_space=pl.ANY)
    output, grad_features, sums = pl.pallas_call(
        functools.partial(main_kernel, n_wide, n_narrow),
        out_shape=(shape((512, 128), BF16), shape((512, 128), BF16), shape((ROWS, 128), F32)),
        in_specs=[large] * 4,
        out_specs=(large, large, inside),
        scratch_shapes=[
            VMEM((512, 128), BF16), VMEM((512, 128), BF16), VMEM((432, 48), BF16), VMEM((432, 32), BF16), dma((4,)),
            VMEM((2, 512, 128), F32), VMEM((16, 512), BF16), VMEM((16, 512), BF16),
            VMEM((2, 768, 128), BF16), VMEM((16, 768), BF16), VMEM((16, 768), BF16), dma((8,)), dma((8,)),
            VMEM((864, 128), F32), VMEM((768, 128), BF16), VMEM((128, 896), BF16), VMEM((160, 512), BF16),
            VMEM((144, 128), BF16), VMEM((32, 144), BF16), VMEM((16, 384), BF16),
            VMEM((3072, 128), BF16), VMEM((3072, 128), BF16), VMEM((576, 128), BF16),
            VMEM((1280, 128), BF16), VMEM((1280, 128), BF16), VMEM((1024, 128), F32),
            VMEM((512, 256), BF16), VMEM((512, 128), F32), VMEM((ROWS, 128), F32),
            VMEM((512, 128), BF16), VMEM((512, 128), BF16), dma((2,)),
            VMEM((g1, depth, 128), F32), VMEM((g1 - 1, depth, 128), F32), VMEM((depth, 128), BF16),
            VMEM((g2, depth, 128), BF16), VMEM((g1, depth, 128), F32),
            dma, dma, dma, dma, dma, dma,
        ],
        compiler_params=pltpu.CompilerParams(
            collective_id=0, has_side_effects=True, vmem_limit_bytes=56 * 1024 * 1024),
        name="levels",
    )(features.reshape(512, 128), cotangent.reshape(512, 128), fw, cw)
    gfine, gcoarse, output, grad_features = pl.pallas_call(
        functools.partial(finish_kernel, 1.0 / math.sqrt(cells), 1.0 / math.sqrt(cells // 8)),
        out_shape=(shape((432, 48), F32), shape((432, 32), F32), shape((512, 128), BF16), shape((512, 128), BF16)),
        in_specs=[large] * 3,
        out_specs=(large,) * 4,
        scratch_shapes=[VMEM((ROWS, 128), F32), VMEM((512, 128), BF16), VMEM((512, 128), BF16),
                        VMEM((432, 48), F32), VMEM((432, 32), F32), dma((11,))],
        name="finish",
    )(sums, output, grad_features)
    return (
        output.reshape(16, 16, 2, 128),
        grad_features.reshape(16, 16, 2, 128),
        jnp.transpose(gfine.reshape(3, 3, 3, 16, 48), (3, 4, 0, 1, 2)),
        jnp.transpose(gcoarse.reshape(3, 3, 3, 16, 32), (4, 3, 0, 1, 2)),
    )


def solution(mesh):
    placed = P(None, "wide", None, "narrow")
    return jax.shard_map(
        functools.partial(shards, mesh.shape["wide"], mesh.shape["narrow"]),
        mesh=mesh,
        in_specs=(placed, placed, P(), P()),
        out_specs=(placed, placed, P(), P()),
        check_vma=False,
    )
```

```python
import functools
import math

import jax
import jax.numpy as jnp
from jax import lax
from jax.experimental import pallas as pl
from jax.experimental.pallas import tpu as pltpu
from jax.sharding import PartitionSpec as P

F32, BF16 = jnp.float32, jnp.bfloat16
MESH = pl.DeviceIdType.MESH
VMEM = pltpu.VMEM
OUTER = 4
ROWS = 192
GRANT = 55040 * 1024


def dot(a, b):
    return lax.dot_general(a, b, (((1,), (0,)), ((), ())), preferred_element_type=F32)


def dot_nt(a, b):
    return lax.dot_general(a, b, (((1,), (1,)), ((), ())), preferred_element_type=F32)


def iota(shape, axis):
    return lax.broadcasted_iota(jnp.int32, shape, axis)


def neighbours(n_wide, n_narrow, me_y, me_x):
    up, down = lax.rem(me_y + n_wide - 1, n_wide), lax.rem(me_y + 1, n_wide)
    west, east = lax.rem(me_x + n_narrow - 1, n_narrow), lax.rem(me_x + 1, n_narrow)
    return [(up, me_x), (down, me_x), (me_y, west), (me_y, east),
            (up, west), (up, east), (down, west), (down, east)]


def pack_own(f_ref, c_ref, ext_ref, wide32, go_left, go_right):
    for k, ref in enumerate((f_ref, c_ref)):
        wide32[k] = ref[...].astype(F32)
        for j in range(32):
            part = wide32[k, pl.ds(j, 16, stride=32), :]
            ext_ref[k, 128 + 16 * j:144 + 16 * j, :] = part.astype(BF16)
    row, col = iota((16, 128), 0), iota((16, 128), 1)
    for start, buf in ((0, go_left), (124, go_right)):
        total = jnp.zeros((16, 512), F32)
        for k in range(2):
            pick = (row >= 4 * k) & (row < 4 * k + 4) & (col == start + row - 4 * k)
            total += dot_nt(pick.astype(F32).astype(BF16), ext_ref[k, 128:640, :])
        buf[...] = total.astype(BF16)


def halo_copies(near, ext_ref, left_ref, right_ref, go_left, go_right, send, recv):
    plan = [
        (ext_ref.at[:, pl.ds(128, 128), :], ext_ref.at[:, pl.ds(640, 128), :]),
        (ext_ref.at[:, pl.ds(512, 128), :], ext_ref.at[:, pl.ds(0, 128), :]),
        (go_left, right_ref.at[:, pl.ds(128, 512)]),
        (go_right, left_ref.at[:, pl.ds(128, 512)]),
        (go_left.at[:, pl.ds(0, 128)], right_ref.at[:, pl.ds(640, 128)]),
        (go_right.at[:, pl.ds(0, 128)], left_ref.at[:, pl.ds(640, 128)]),
        (go_left.at[:, pl.ds(384, 128)], right_ref.at[:, pl.ds(0, 128)]),
        (go_right.at[:, pl.ds(384, 128)], left_ref.at[:, pl.ds(0, 128)]),
    ]
    return [
        pltpu.make_async_remote_copy(
            src_ref=src, dst_ref=dst, send_sem=send.at[j], recv_sem=recv.at[j],
            device_id=near[j], device_id_type=MESH)
        for j, (src, dst) in enumerate(plan)
    ]


def prepare_weights(fw_ref, cw_ref, wide_w, stack, w_fwd, w_bwd, stack_c, w_pre, w_gp):
    lane = iota((16, 128), 1)
    wide_w[...] = jnp.zeros_like(wide_w)
    wide_w[0:432, 0:48] = fw_ref[...].astype(F32)
    wide_w[432:864, 0:32] = cw_ref[...].astype(F32)

    def tap(ky, kz, kx):
        at = ((ky * 3 + kz) * 3 + kx) * 16
        return wide_w[at:at + 16, :]

    zero16 = jnp.zeros((16, 128), BF16)
    for z in range(2):
        for ky in range(3):
            base = jnp.zeros((16, 128), F32)
            for kx in range(3):
                for zz in range(2):
                    at = 32 * kx + 16 * zz
                    moved = tap(ky, zz - z + 1, kx)
                    if at:
                        moved = pltpu.roll(moved, at, 1)
                    base = jnp.where((lane >= at) & (lane < at + 16), moved, base)
            for px in range(2):
                block = (pltpu.roll(base, 32, 1) if px else base).astype(BF16)
                for py in range(2):
                    rows = (py * 2 + px) * 32 + z * 16
                    w_fwd[rows:rows + 16, (ky + py) * 128:(ky + py + 1) * 128] = block
    for py in range(2):
        idle = 3 if py == 0 else 0
        for blocks in range(4):
            rows = py * 64 + blocks * 16
            w_fwd[rows:rows + 16, idle * 128:(idle + 1) * 128] = zero16
    spans = {(0, 0): (0,), (0, 1): (1, 2), (0, 2): (), (1, 0): (), (1, 1): (0, 1), (1, 2): (2,)}
    for z in range(2):
        pair = [[tap(ky, 1 - z, kx) + tap(ky, 2 - z, kx) for kx in range(3)] for ky in range(3)]
        for py in range(2):
            for dy in range(3):
                kys = spans[py, dy]
                for px in range(2):
                    rows = (py * 2 + px) * 32 + z * 16
                    block = jnp.zeros((16, 128), F32)
                    for dx in range(3):
                        terms = [pair[ky][kx] for ky in kys for kx in spans[px, dx]]
                        if not terms:
                            continue
                        moved = pltpu.roll(functools.reduce(jnp.add, terms), (32 * dx - 16) % 128, 1)
                        block = jnp.where((lane >= 32 * dx) & (lane < 32 * dx + 32), moved, block)
                    w_fwd[rows:rows + 16, 512 + dy * 128:512 + (dy + 1) * 128] = block.astype(BF16)
    for z in range(2):
        for ky in range(3):
            for wx in range(4):
                for zz in range(2):
                    at = (z * 3 + ky) * 128 + wx * 32 + zz * 16
                    if wx == 3:
                        stack[at:at + 16, :] = zero16
                    else:
                        stack[at:at + 16, :] = tap(2 - ky, 1 + z - zz, 2 - wx).astype(BF16)
    eye = (iota((48, 128), 0) == iota((48, 128), 1)).astype(F32).astype(BF16)
    turned = dot_nt(eye, stack[...])
    w_bwd[...] = jnp.zeros_like(w_bwd)
    act = [jnp.zeros((32, 128), F32) for _ in range(4)]
    for z in range(2):
        for ky in range(3):
            at = (z * 3 + ky) * 128
            base = turned[:, at:at + 128]
            for px in range(2):
                moved = pltpu.roll(base, 32, 1) if px else base
                for py in range(2):
                    rows = (py * 2 + px) * 32 + z * 16
                    w_bwd[rows:rows + 16, (ky + py) * 128:(ky + py + 1) * 128] = moved[0:16].astype(BF16)
                    act[ky + py] = act[ky + py] + moved[16:48]
    for wy in range(4):
        w_bwd[128:160, wy * 128:(wy + 1) * 128] = act[wy].astype(BF16)
    for dy in range(3):
        block = jnp.zeros((16, 128), F32)
        for dx in range(3):
            at = 432 + ((dy * 3 + 1) * 3 + dx) * 16
            stack_c[(dy * 3 + dx) * 16:(dy * 3 + dx + 1) * 16, :] = wide_w[at:at + 16, :].astype(BF16)
            at = 432 + (((2 - dy) * 3 + 1) * 3 + 2 - dx) * 16
            moved = wide_w[at:at + 16, :]
            if dx:
                moved = pltpu.roll(moved, 32 * dx, 1)
            block = jnp.where((lane >= 32 * dx) & (lane < 32 * dx + 32), moved, block)
        w_gp[:, dy * 128:(dy + 1) * 128] = block.astype(BF16)
    w_pre[...] = dot_nt(eye[0:32], stack_c[...]).astype(BF16)


def level_gradients(n_wide, n_narrow, me_y, me_x, ext_ref, left_ref, right_ref, sums_ref,
                    w_bwd, w_pre, fine, cot, pool, act, gpre, keep_gj, sums):
    top, bottom = me_y > 0, me_y < n_wide - 1
    first, last = me_x > 0, me_x < n_narrow - 1

    want = iota((128, 512), 1)
    want = 2 * ((want & 127) - 2) - 1 + (want >> 7)
    spread = (iota((128, 512), 0) == want).astype(F32).astype(BF16)
    side_want = iota((32, 512), 1)
    side_want = 2 * ((side_want & 127) - 2) - 1 + (side_want >> 7)
    side_row = iota((32, 512), 0)
    sides = jnp.concatenate([left_ref[...].astype(F32), right_ref[...].astype(F32)], axis=0)
    turned = jnp.transpose(sides).astype(BF16)
    for k, field in enumerate((fine, cot)):
        west = (side_row >= 4 * k) & (side_row < 4 * k + 4) & (side_want == side_row - 4 * k - 4) & first
        east = (side_row >= 16 + 4 * k) & (side_row < 20 + 4 * k) & (side_want == side_row - 16 - 4 * k + 128) & last
        both = jnp.concatenate([spread, (west | east).astype(F32).astype(BF16)], axis=0)
        for part in range(6):
            at = part * 128
            got = dot(jnp.concatenate([ext_ref[k, at:at + 128, :], turned[at:at + 128, :]], axis=1), both)
            if part == 0:
                got = jnp.where(top, got, 0.0)
            if part == 5:
                got = jnp.where(bottom, got, 0.0)
            got = got.astype(BF16)
            for y in range(4):
                for wx in range(4):
                    to = (part * 4 + y) * 128 + wx * 32
                    field[to:to + 32, :] = got[y * 32:y * 32 + 32, wx * 128:wx * 128 + 128]

    for r in range(12):
        both = (fine[2 * r * 128 + 32:2 * r * 128 + 96, :].astype(F32)
                + fine[(2 * r + 1) * 128 + 32:(2 * r + 1) * 128 + 96, :].astype(F32))
        mean = (both[0:16] + both[16:32] + both[32:48] + both[48:64]) * 0.125
        pool[r * 48:r * 48 + 16, :] = pltpu.roll(mean, 1, 1).astype(BF16)
        pool[r * 48 + 16:r * 48 + 32, :] = mean.astype(BF16)
        pool[r * 48 + 32:r * 48 + 48, :] = pltpu.roll(mean, 127, 1).astype(BF16)

    lane = iota((32, 128), 1)
    inside = ((lane >= 2) | ((lane == 1) & first)) & ((lane <= 65) | ((lane == 66) & last))
    own = (iota((128, 128), 1) >= 2) & (iota((128, 128), 1) <= 65)
    blank = jnp.zeros((32, 128), BF16)
    for r in range(1, 11):
        pre = dot(w_pre[...], pool[(r - 1) * 48:(r + 2) * 48, :])
        sig = 1.0 / (1.0 + jnp.exp(-pre))
        back = dot(w_bwd[...], cot[(2 * r - 1) * 128:(2 * r + 3) * 128, :])
        grad_act = back[128:160].astype(BF16).astype(F32)
        slope = grad_act * (sig * (1.0 + pre * (1.0 - sig)))
        valid = inside
        if r == 1:
            valid = inside & top
        if r == 10:
            valid = inside & bottom
        for value, to in ((pre * sig, act), (slope, gpre)):
            value = jnp.where(valid, value, 0.0)
            at = (r - 1) * 128
            to[at:at + 32, :] = pltpu.roll(value, 1, 1).astype(BF16)
            to[at + 32:at + 64, :] = value.astype(BF16)
            to[at + 64:at + 96, :] = pltpu.roll(value, 127, 1).astype(BF16)
            to[at + 96:at + 128, :] = blank
        if 2 <= r <= 9:
            keep_gj[(r - 2) * 128:(r - 1) * 128, :] = back[0:128]

    def own_cot(r):
        a, b = 2 * r * 128, (2 * r + 1) * 128
        both = jnp.concatenate([cot[a + 32:a + 96, :], cot[b + 32:b + 96, :]], axis=0)
        return jnp.where(own, both.astype(F32), 0.0).astype(BF16)

    def lanes(parts):
        return jnp.concatenate(parts, axis=1)

    rows = range(2, 10)
    lhs = lanes([own_cot(r) for r in rows])
    grad = dot_nt(lhs, lanes([fine[(2 * r - 1) * 128:(2 * r + 3) * 128, :] for r in rows]))
    grad_up = dot_nt(lhs, lanes([act[(r - 2) * 128:(r + 1) * 128, :] for r in rows]))
    grad_c = dot_nt(
        lanes([pool[(r - 1) * 48:(r + 2) * 48, :] for r in rows]),
        lanes([jnp.where(own[0:32], gpre[(r - 1) * 128 + 32:(r - 1) * 128 + 64, :].astype(F32), 0.0).astype(BF16)
               for r in rows]))
    dys = ((0, 1, 1), (1, 1, 2))
    taps = [jnp.concatenate([grad_c[t * 16:t * 16 + 16], jnp.zeros((16, 96), F32)], axis=1) for t in range(9)]
    none = jnp.zeros((16, 128), F32)
    for block in range(6):
        if block < 3:
            ky = block
            total = sum(grad[py * 64:py * 64 + 32, (ky + py) * 128:(ky + py + 1) * 128] for py in range(2))
            odd = sum(grad[py * 64 + 32:py * 64 + 64, (ky + py) * 128:(ky + py + 1) * 128] for py in range(2))
            total = total + pltpu.roll(odd, 96, 1)
        else:
            ky = block - 3
            even, odd = (sum(grad_up[py * 64 + px * 32:py * 64 + px * 32 + 32, dys[py][ky] * 128:(dys[py][ky] + 1) * 128]
                             for py in range(2)) for px in range(2))
            total = jnp.where(lane < 64, even, pltpu.roll(even, 32, 1)) + jnp.where(lane < 32, pltpu.roll(odd, 96, 1), odd)
        extra = jnp.concatenate([taps[t] if t < 9 else none for t in (2 * block, 2 * block + 1)], axis=0)
        sums[block * 32:block * 32 + 32, :] = jnp.where(lane < 96, total, pltpu.roll(extra, 96, 1))
    count, depth = sums_ref.shape[0], sums_ref.shape[1]
    for j in range(count):
        sums_ref[j] = sums[j * depth:(j + 1) * depth, :].astype(sums_ref.dtype)


def level_outputs(out_ref, gf_ref, w_fwd, w_gp, fine, act, gpre, keep_gj, flat, turn):
    joiner = iota((256, 128), 0)
    joiner = (2 * ((joiner & 127) - 2) + (joiner >> 7) == iota((256, 128), 1)).astype(F32).astype(BF16)

    def place(values, r):
        values = values.astype(BF16)
        for py in range(2):
            at = (2 * (r - 2) + py) * 32
            flat[at:at + 32, 0:128] = values[py * 64:py * 64 + 32]
            flat[at:at + 32, 128:256] = values[py * 64 + 32:py * 64 + 64]

    def finish(to):
        for part in range(4):
            joined = dot(flat[part * 128:part * 128 + 128, :], joiner)
            for j in range(8):
                turn[pl.ds(part * 8 + j, 16, stride=32), :] = joined[j * 16:j * 16 + 16]
        to[...] = turn[...].astype(BF16)

    for r in range(2, 10):
        got = dot(w_fwd[:, 0:512], fine[(2 * r - 1) * 128:(2 * r + 3) * 128, :])
        got += dot(w_fwd[:, 512:896], act[(r - 2) * 128:(r + 1) * 128, :])
        place(got, r)
    finish(out_ref)
    for r in range(2, 10):
        low = dot(w_gp[...], gpre[(r - 2) * 128:(r + 1) * 128, :]).astype(BF16).astype(F32) * 0.125
        place(keep_gj[(r - 2) * 128:(r - 1) * 128, :] + jnp.concatenate([low] * 8, axis=0), r)
    finish(gf_ref)


def main_kernel(n_wide, n_narrow, f_hbm, c_hbm, fw_hbm, cw_hbm, out_hbm, gf_hbm, total_ref,
                f_ref, c_ref, fw_ref, cw_ref, in_sem,
                wide32, go_left, go_right, ext, left, right, halo_send, halo_recv,
                wide_w, stack, w_fwd, w_bwd, stack_c, w_pre, w_gp,
                fine, cot, pool, act, gpre, keep_gj, flat, turn, sums,
                out_v, gf_v, out_sem, mine, got1, part, got2, fin, send1, recv1, send2, recv2, send3, recv3):
    g1, g2 = n_wide // OUTER, n_narrow * OUTER
    depth = ROWS // g1
    len_y, len_z, len_x = g1 // 2, 2 * OUTER, n_narrow // 2
    me_y, me_x = lax.axis_index("wide"), lax.axis_index("narrow")
    me1 = lax.rem(me_y, g1)
    run_z = lax.div(me_y, g1)
    at_y, at_core = lax.div(me1, 2), lax.rem(me1, 2)
    at_z, at_x = lax.rem(me_x, 2) * OUTER + run_z, lax.div(me_x, 2)
    me2 = at_x * len_z + at_z

    def far_first(sizes):
        steps = [(a, b) for a in range(sizes[0]) for b in range(sizes[1]) if a or b]
        return sorted(steps, key=lambda s: -sum(min(k, n - k) for k, n in zip(s, sizes)))

    first, second = [], []
    for dy, dcore in far_first((len_y, 2)):
        k = lax.rem(at_y + dy, len_y) * 2 + lax.rem(at_core + dcore, 2)
        first.append((k, (run_z * g1 + k, me_x)))
    for dz, dx in far_first((len_z, len_x)):
        z, x = lax.rem(at_z + dz, len_z), lax.rem(at_x + dx, len_x)
        second.append((x * len_z + z, (lax.rem(z, OUTER) * g1 + me1, x * 2 + lax.div(z, OUTER))))

    barrier = pltpu.get_barrier_semaphore()
    near = neighbours(n_wide, n_narrow, me_y, me_x)
    for device in near + [device for _, device in second + first]:
        pl.semaphore_signal(barrier, inc=1, device_id=device, device_id_type=MESH)
    reads = [pltpu.make_async_copy(src, dst, in_sem.at[j]) for j, (src, dst) in enumerate(
        ((f_hbm, f_ref), (c_hbm, c_ref), (fw_hbm, fw_ref), (cw_hbm, cw_ref)))]
    for read in reads:
        read.start()
    for read in reads[:2]:
        read.wait()
    pack_own(f_ref, c_ref, ext, wide32, go_left, go_right)
    pl.semaphore_wait(barrier, 8 + g1 + g2 - 2)
    halo = halo_copies(near, ext, left, right, go_left, go_right, halo_send, halo_recv)
    for j in (4, 5, 6, 7, 2, 3, 0, 1):
        halo[j].start()
    for read in reads[2:]:
        read.wait()
    prepare_weights(fw_ref, cw_ref, wide_w, stack, w_fwd, w_bwd, stack_c, w_pre, w_gp)
    for copy in halo:
        copy.wait_recv()
    level_gradients(n_wide, n_narrow, me_y, me_x, ext, left, right, mine,
                    w_bwd, w_pre, fine, cot, pool, act, gpre, keep_gj, sums)

    def send_all(group, source, slot, sends, receives):
        for j, (k, device) in enumerate(group):
            pltpu.make_async_remote_copy(
                src_ref=source(k), dst_ref=slot(j), send_sem=sends, recv_sem=receives,
                device_id=device, device_id_type=MESH).start()

    def all_of(ref, sends, receives):
        return pltpu.make_async_remote_copy(
            src_ref=ref, dst_ref=ref, send_sem=sends, recv_sem=receives,
            device_id=near[0], device_id_type=MESH)

    one = all_of(got1, send1, recv1)
    two = all_of(got2.at[pl.ds(0, g2 - 1)], send2, recv2)
    three = all_of(fin.at[pl.ds(0, g1 - 1)], send3, recv3)
    send_all(first, lambda k: mine.at[k], lambda j: got1.at[j], send1, recv1)
    level_outputs(out_v, gf_v, w_fwd, w_gp, fine, act, gpre, keep_gj, flat, turn)
    writes = [pltpu.make_async_copy(out_v, out_hbm, out_sem.at[0]), pltpu.make_async_copy(gf_v, gf_hbm, out_sem.at[1])]
    for write in writes:
        write.start()
    one.wait_recv()
    total = mine[me1].astype(F32)
    for j in range(g1 - 1):
        total += got1[j].astype(F32)
    part[...] = total.astype(part.dtype)
    send_all(second, lambda k: part, lambda j: got2.at[me2], send2, recv2)
    got2[me2] = part[...]
    for copy in halo:
        copy.wait_send()
    one.wait_send()
    for write in writes:
        write.wait()
    two.wait_recv()
    total = got2[0].astype(F32)
    for k in range(1, g2):
        total += got2[k].astype(F32)
    fin[me1] = total.astype(fin.dtype)
    send_all(first, lambda k: fin.at[me1], lambda j: fin.at[me1], send3, recv3)
    two.wait_send()
    three.wait_recv()
    for j in range(g1):
        total_ref[j * depth:(j + 1) * depth, :] = fin[j].astype(F32)
    three.wait_send()


def finish_kernel(scale_fine, scale_coarse, turn, out_in, gf_in, gfine_out, gcoarse_out, out_ref, gf_ref,
                  out_v, gf_v, gfine_ref, gcoarse_ref, sem):
    def copy(src, dst, j):
        return pltpu.make_async_copy(src, dst, sem.at[j])

    reads = [copy(out_in, out_v, 1), copy(gf_in, gf_v, 2)]
    writes = [copy(out_v, out_ref, 3), copy(gf_v, gf_ref, 4)]
    for read in reads:
        read.start()
    lane = iota((16, 128), 1)
    for ky in range(3):
        if ky:
            reads[ky - 1].wait()
            writes[ky - 1].start()
        flow = [turn[ky * 32 + z * 16:ky * 32 + z * 16 + 16, :] for z in range(2)]
        rise = [turn[96 + ky * 32 + z * 16:96 + ky * 32 + z * 16 + 16, :] for z in range(2)]
        ups = (rise[1], rise[0] + rise[1], rise[0])
        for kx in range(3):
            near0 = [pltpu.roll(flow[z], (-32 * kx) % 128, 1) if kx else flow[z] for z in range(2)]
            near1 = [pltpu.roll(flow[z], (-32 * kx - 16) % 128, 1) for z in range(2)]
            own = (near0[1], near0[0] + near1[1], near1[0])
            for kz in range(3):
                whole = jnp.where(lane < 16, own[kz], pltpu.roll(ups[kz], (16 - 32 * kx) % 128, 1))
                at = ((ky * 3 + kz) * 3 + kx) * 16
                gfine_ref[at:at + 16, :] = (whole * scale_fine)[:, 0:48]
                if kz == 1:
                    t = ky * 3 + kx
                    row = (t // 2) * 32 + (t % 2) * 16
                    coarse = pltpu.roll(turn[row:row + 16, :], 32, 1)[:, 0:32] * scale_coarse
                    gcoarse_ref[at:at + 16, :] = coarse
                else:
                    gcoarse_ref[at:at + 16, :] = jnp.zeros((16, 32), F32)
        for j, (src, dst) in enumerate(((gfine_ref, gfine_out), (gcoarse_ref, gcoarse_out))):
            rows = pl.ds(ky * 144, 144)
            writes.append(copy(src.at[rows, :], dst.at[rows, :], 5 + 2 * ky + j))
            writes[-1].start()
    for write in writes:
        write.wait()


def shards(n_wide, n_narrow, features, cotangent, coarse_weight, fine_weight):
    inside = pl.BlockSpec(memory_space=VMEM)
    shape = jax.ShapeDtypeStruct
    g1, g2 = n_wide // OUTER, n_narrow * OUTER
    depth = ROWS // g1
    cells = n_wide * 16 * 2 * n_narrow * 128
    fw = jnp.transpose(fine_weight, (2, 3, 4, 0, 1)).reshape(432, 48)
    cw = jnp.transpose(coarse_weight, (2, 3, 4, 1, 0)).reshape(432, 32)
    dma = pltpu.SemaphoreType.DMA
    large = pl.BlockSpec(memory_space=pltpu.HBM)
    output, grad_features, sums = pl.pallas_call(
        functools.partial(main_kernel, n_wide, n_narrow),
        out_shape=(shape((512, 128), BF16), shape((512, 128), BF16), shape((ROWS, 128), F32)),
        in_specs=[large] * 4,
        out_specs=(large, large, inside),
        scratch_shapes=[
            VMEM((512, 128), BF16), VMEM((512, 128), BF16), VMEM((432, 48), BF16), VMEM((432, 32), BF16), dma((4,)),
            VMEM((2, 512, 128), F32), VMEM((16, 512), BF16), VMEM((16, 512), BF16),
            VMEM((2, 768, 128), BF16), VMEM((16, 768), BF16), VMEM((16, 768), BF16), dma((8,)), dma((8,)),
            VMEM((864, 128), F32), VMEM((768, 128), BF16), VMEM((128, 896), BF16), VMEM((160, 512), BF16),
            VMEM((144, 128), BF16), VMEM((32, 144), BF16), VMEM((16, 384), BF16),
            VMEM((3072, 128), BF16), VMEM((3072, 128), BF16), VMEM((576, 128), BF16),
            VMEM((1280, 128), BF16), VMEM((1280, 128), BF16), VMEM((1024, 128), F32),
            VMEM((512, 256), BF16), VMEM((512, 128), F32), VMEM((ROWS, 128), F32),
            VMEM((512, 128), BF16), VMEM((512, 128), BF16), dma((2,)),
            VMEM((g1, depth, 128), F32), VMEM((g1 - 1, depth, 128), F32), VMEM((depth, 128), BF16),
            VMEM((g2, depth, 128), BF16), VMEM((g1, depth, 128), F32),
            dma, dma, dma, dma, dma, dma,
        ],
        compiler_params=pltpu.CompilerParams(
            collective_id=0, has_side_effects=True, vmem_limit_bytes=GRANT),
        name="levels",
    )(features.reshape(512, 128), cotangent.reshape(512, 128), fw, cw)
    gfine, gcoarse, output, grad_features = pl.pallas_call(
        functools.partial(finish_kernel, 1.0 / math.sqrt(cells), 1.0 / math.sqrt(cells // 8)),
        out_shape=(shape((432, 48), F32), shape((432, 32), F32), shape((512, 128), BF16), shape((512, 128), BF16)),
        in_specs=[inside, large, large],
        out_specs=(large,) * 4,
        scratch_shapes=[VMEM((512, 128), BF16), VMEM((512, 128), BF16),
                        VMEM((432, 48), F32), VMEM((432, 32), F32), dma((11,))],
        compiler_params=pltpu.CompilerParams(vmem_limit_bytes=GRANT),
        name="finish",
    )(sums, output, grad_features)
    return (
        output.reshape(16, 16, 2, 128),
        grad_features.reshape(16, 16, 2, 128),
        jnp.transpose(gfine.reshape(3, 3, 3, 16, 48), (3, 4, 0, 1, 2)),
        jnp.transpose(gcoarse.reshape(3, 3, 3, 16, 32), (4, 3, 0, 1, 2)),
    )


def solution(mesh):
    placed = P(None, "wide", None, "narrow")
    return jax.shard_map(
        functools.partial(shards, mesh.shape["wide"], mesh.shape["narrow"]),
        mesh=mesh,
        in_specs=(placed, placed, P(), P()),
        out_specs=(placed, placed, P(), P()),
        check_vma=False,
    )
```

```python
import functools
import math

import jax
import jax.numpy as jnp
from jax import lax
from jax.experimental import pallas as pl
from jax.experimental.pallas import tpu as pltpu
from jax.sharding import PartitionSpec as P

F32, BF16 = jnp.float32, jnp.bfloat16
MESH = pl.DeviceIdType.MESH
VMEM = pltpu.VMEM
OUTER = 4
ROWS = 192
GRANT = 55040 * 1024


def dot(a, b):
    return lax.dot_general(a, b, (((1,), (0,)), ((), ())), preferred_element_type=F32)


def dot_nt(a, b):
    return lax.dot_general(a, b, (((1,), (1,)), ((), ())), preferred_element_type=F32)


def iota(shape, axis):
    return lax.broadcasted_iota(jnp.int32, shape, axis)


def neighbours(n_wide, n_narrow, me_y, me_x):
    up, down = lax.rem(me_y + n_wide - 1, n_wide), lax.rem(me_y + 1, n_wide)
    west, east = lax.rem(me_x + n_narrow - 1, n_narrow), lax.rem(me_x + 1, n_narrow)
    return [(up, me_x), (down, me_x), (me_y, west), (me_y, east),
            (up, west), (up, east), (down, west), (down, east)]


def pack_own(f_ref, c_ref, ext_ref, wide32, go_left, go_right):
    for k, ref in enumerate((f_ref, c_ref)):
        wide32[k] = ref[...].astype(F32)
        for j in range(32):
            part = wide32[k, pl.ds(j, 16, stride=32), :]
            ext_ref[k, 128 + 16 * j:144 + 16 * j, :] = part.astype(BF16)
    row, col = iota((16, 128), 0), iota((16, 128), 1)
    for start, buf in ((0, go_left), (124, go_right)):
        total = jnp.zeros((16, 512), F32)
        for k in range(2):
            pick = (row >= 4 * k) & (row < 4 * k + 4) & (col == start + row - 4 * k)
            total += dot_nt(pick.astype(F32).astype(BF16), ext_ref[k, 128:640, :])
        buf[...] = total.astype(BF16)


def halo_copies(near, ext_ref, left_ref, right_ref, go_left, go_right, send, recv):
    plan = [
        (ext_ref.at[:, pl.ds(128, 128), :], ext_ref.at[:, pl.ds(640, 128), :]),
        (ext_ref.at[:, pl.ds(512, 128), :], ext_ref.at[:, pl.ds(0, 128), :]),
        (go_left, right_ref.at[:, pl.ds(128, 512)]),
        (go_right, left_ref.at[:, pl.ds(128, 512)]),
        (go_left.at[:, pl.ds(0, 128)], right_ref.at[:, pl.ds(640, 128)]),
        (go_right.at[:, pl.ds(0, 128)], left_ref.at[:, pl.ds(640, 128)]),
        (go_left.at[:, pl.ds(384, 128)], right_ref.at[:, pl.ds(0, 128)]),
        (go_right.at[:, pl.ds(384, 128)], left_ref.at[:, pl.ds(0, 128)]),
    ]
    return [
        pltpu.make_async_remote_copy(
            src_ref=src, dst_ref=dst, send_sem=send.at[j], recv_sem=recv.at[j],
            device_id=near[j], device_id_type=MESH)
        for j, (src, dst) in enumerate(plan)
    ]


def prepare_weights(fw_ref, cw_ref, wide_w, stack, w_fwd, w_bwd, stack_c, w_pre, w_gp):
    lane = iota((16, 128), 1)
    wide_w[...] = jnp.zeros_like(wide_w)
    wide_w[0:432, 0:48] = fw_ref[...].astype(F32)
    wide_w[432:864, 0:32] = cw_ref[...].astype(F32)

    def tap(ky, kz, kx):
        at = ((ky * 3 + kz) * 3 + kx) * 16
        return wide_w[at:at + 16, :]

    zero16 = jnp.zeros((16, 128), BF16)
    for z in range(2):
        for ky in range(3):
            base = jnp.zeros((16, 128), F32)
            for kx in range(3):
                for zz in range(2):
                    at = 32 * kx + 16 * zz
                    moved = tap(ky, zz - z + 1, kx)
                    if at:
                        moved = pltpu.roll(moved, at, 1)
                    base = jnp.where((lane >= at) & (lane < at + 16), moved, base)
            for px in range(2):
                block = (pltpu.roll(base, 32, 1) if px else base).astype(BF16)
                for py in range(2):
                    rows = (py * 2 + px) * 32 + z * 16
                    w_fwd[rows:rows + 16, (ky + py) * 128:(ky + py + 1) * 128] = block
    for py in range(2):
        idle = 3 if py == 0 else 0
        for blocks in range(4):
            rows = py * 64 + blocks * 16
            w_fwd[rows:rows + 16, idle * 128:(idle + 1) * 128] = zero16
    spans = {(0, 0): (0,), (0, 1): (1, 2), (0, 2): (), (1, 0): (), (1, 1): (0, 1), (1, 2): (2,)}
    for z in range(2):
        pair = [[tap(ky, 1 - z, kx) + tap(ky, 2 - z, kx) for kx in range(3)] for ky in range(3)]
        for py in range(2):
            for dy in range(3):
                kys = spans[py, dy]
                for px in range(2):
                    rows = (py * 2 + px) * 32 + z * 16
                    block = jnp.zeros((16, 128), F32)
                    for dx in range(3):
                        terms = [pair[ky][kx] for ky in kys for kx in spans[px, dx]]
                        if not terms:
                            continue
                        moved = pltpu.roll(functools.reduce(jnp.add, terms), (32 * dx - 16) % 128, 1)
                        block = jnp.where((lane >= 32 * dx) & (lane < 32 * dx + 32), moved, block)
                    w_fwd[rows:rows + 16, 512 + dy * 128:512 + (dy + 1) * 128] = block.astype(BF16)
    for z in range(2):
        for ky in range(3):
            for wx in range(4):
                for zz in range(2):
                    at = (z * 3 + ky) * 128 + wx * 32 + zz * 16
                    if wx == 3:
                        stack[at:at + 16, :] = zero16
                    else:
                        stack[at:at + 16, :] = tap(2 - ky, 1 + z - zz, 2 - wx).astype(BF16)
    eye = (iota((48, 128), 0) == iota((48, 128), 1)).astype(F32).astype(BF16)
    turned = dot_nt(eye, stack[...])
    w_bwd[...] = jnp.zeros_like(w_bwd)
    act = [jnp.zeros((32, 128), F32) for _ in range(4)]
    for z in range(2):
        for ky in range(3):
            at = (z * 3 + ky) * 128
            base = turned[:, at:at + 128]
            for px in range(2):
                moved = pltpu.roll(base, 32, 1) if px else base
                for py in range(2):
                    rows = (py * 2 + px) * 32 + z * 16
                    w_bwd[rows:rows + 16, (ky + py) * 128:(ky + py + 1) * 128] = moved[0:16].astype(BF16)
                    act[ky + py] = act[ky + py] + moved[16:48]
    for wy in range(4):
        w_bwd[128:160, wy * 128:(wy + 1) * 128] = act[wy].astype(BF16)
    for dy in range(3):
        block = jnp.zeros((16, 128), F32)
        for dx in range(3):
            at = 432 + ((dy * 3 + 1) * 3 + dx) * 16
            stack_c[(dy * 3 + dx) * 16:(dy * 3 + dx + 1) * 16, :] = wide_w[at:at + 16, :].astype(BF16)
            at = 432 + (((2 - dy) * 3 + 1) * 3 + 2 - dx) * 16
            moved = wide_w[at:at + 16, :]
            if dx:
                moved = pltpu.roll(moved, 32 * dx, 1)
            block = jnp.where((lane >= 32 * dx) & (lane < 32 * dx + 32), moved, block)
        w_gp[:, dy * 128:(dy + 1) * 128] = block.astype(BF16)
    w_pre[...] = dot_nt(eye[0:32], stack_c[...]).astype(BF16)


def level_gradients(n_wide, n_narrow, me_y, me_x, ext_ref, left_ref, right_ref, sums_ref,
                    w_bwd, w_pre, fine, cot, pool, act, gpre, keep_gj, sums):
    top, bottom = me_y > 0, me_y < n_wide - 1
    first, last = me_x > 0, me_x < n_narrow - 1

    want = iota((128, 512), 1)
    want = 2 * ((want & 127) - 2) - 1 + (want >> 7)
    spread = (iota((128, 512), 0) == want).astype(F32).astype(BF16)
    side_want = iota((32, 512), 1)
    side_want = 2 * ((side_want & 127) - 2) - 1 + (side_want >> 7)
    side_row = iota((32, 512), 0)
    sides = jnp.concatenate([left_ref[...].astype(F32), right_ref[...].astype(F32)], axis=0)
    turned = jnp.transpose(sides).astype(BF16)
    for k, field in enumerate((fine, cot)):
        west = (side_row >= 4 * k) & (side_row < 4 * k + 4) & (side_want == side_row - 4 * k - 4) & first
        east = (side_row >= 16 + 4 * k) & (side_row < 20 + 4 * k) & (side_want == side_row - 16 - 4 * k + 128) & last
        both = jnp.concatenate([spread, (west | east).astype(F32).astype(BF16)], axis=0)
        for part in range(6):
            at = part * 128
            got = dot(jnp.concatenate([ext_ref[k, at:at + 128, :], turned[at:at + 128, :]], axis=1), both)
            if part == 0:
                got = jnp.where(top, got, 0.0)
            if part == 5:
                got = jnp.where(bottom, got, 0.0)
            got = got.astype(BF16)
            for y in range(4):
                for wx in range(4):
                    to = (part * 4 + y) * 128 + wx * 32
                    field[to:to + 32, :] = got[y * 32:y * 32 + 32, wx * 128:wx * 128 + 128]

    for r in range(12):
        both = (fine[2 * r * 128 + 32:2 * r * 128 + 96, :].astype(F32)
                + fine[(2 * r + 1) * 128 + 32:(2 * r + 1) * 128 + 96, :].astype(F32))
        mean = (both[0:16] + both[16:32] + both[32:48] + both[48:64]) * 0.125
        pool[r * 48:r * 48 + 16, :] = pltpu.roll(mean, 1, 1).astype(BF16)
        pool[r * 48 + 16:r * 48 + 32, :] = mean.astype(BF16)
        pool[r * 48 + 32:r * 48 + 48, :] = pltpu.roll(mean, 127, 1).astype(BF16)

    lane = iota((32, 128), 1)
    inside = ((lane >= 2) | ((lane == 1) & first)) & ((lane <= 65) | ((lane == 66) & last))
    own = (iota((128, 128), 1) >= 2) & (iota((128, 128), 1) <= 65)
    blank = jnp.zeros((32, 128), BF16)

    def own_cot(r):
        a, b = 2 * r * 128, (2 * r + 1) * 128
        both = jnp.concatenate([cot[a + 32:a + 96, :], cot[b + 32:b + 96, :]], axis=0)
        return jnp.where(own, both.astype(F32), 0.0).astype(BF16)

    def lanes(parts):
        return jnp.concatenate(parts, axis=1)

    grad = jnp.zeros((128, 512), F32)
    for r in range(1, 11):
        pre = dot(w_pre[...], pool[(r - 1) * 48:(r + 2) * 48, :])
        sig = 1.0 / (1.0 + jnp.exp(-pre))
        back = dot(w_bwd[...], cot[(2 * r - 1) * 128:(2 * r + 3) * 128, :])
        grad_act = back[128:160].astype(BF16).astype(F32)
        slope = grad_act * (sig * (1.0 + pre * (1.0 - sig)))
        valid = inside
        if r == 1:
            valid = inside & top
        if r == 10:
            valid = inside & bottom
        for value, to in ((pre * sig, act), (slope, gpre)):
            value = jnp.where(valid, value, 0.0)
            at = (r - 1) * 128
            to[at:at + 32, :] = pltpu.roll(value, 1, 1).astype(BF16)
            to[at + 32:at + 64, :] = value.astype(BF16)
            to[at + 64:at + 96, :] = pltpu.roll(value, 127, 1).astype(BF16)
            to[at + 96:at + 128, :] = blank
        if 2 <= r <= 9:
            keep_gj[(r - 2) * 128:(r - 1) * 128, :] = back[0:128]
        if r in (4, 8):
            four = range(r - 2, r + 2)
            grad += dot_nt(lanes([own_cot(q) for q in four]),
                           lanes([fine[(2 * q - 1) * 128:(2 * q + 3) * 128, :] for q in four]))

    rows = range(2, 10)
    lhs = lanes([own_cot(r) for r in rows])
    grad_up = dot_nt(lhs, lanes([act[(r - 2) * 128:(r + 1) * 128, :] for r in rows]))
    grad_c = dot_nt(
        lanes([pool[(r - 1) * 48:(r + 2) * 48, :] for r in rows]),
        lanes([jnp.where(own[0:32], gpre[(r - 1) * 128 + 32:(r - 1) * 128 + 64, :].astype(F32), 0.0).astype(BF16)
               for r in rows]))
    dys = ((0, 1, 1), (1, 1, 2))
    taps = [jnp.concatenate([grad_c[t * 16:t * 16 + 16], jnp.zeros((16, 96), F32)], axis=1) for t in range(9)]
    none = jnp.zeros((16, 128), F32)
    for block in range(6):
        if block < 3:
            ky = block
            total = sum(grad[py * 64:py * 64 + 32, (ky + py) * 128:(ky + py + 1) * 128] for py in range(2))
            odd = sum(grad[py * 64 + 32:py * 64 + 64, (ky + py) * 128:(ky + py + 1) * 128] for py in range(2))
            total = total + pltpu.roll(odd, 96, 1)
        else:
            ky = block - 3
            even, odd = (sum(grad_up[py * 64 + px * 32:py * 64 + px * 32 + 32, dys[py][ky] * 128:(dys[py][ky] + 1) * 128]
                             for py in range(2)) for px in range(2))
            total = jnp.where(lane < 64, even, pltpu.roll(even, 32, 1)) + jnp.where(lane < 32, pltpu.roll(odd, 96, 1), odd)
        extra = jnp.concatenate([taps[t] if t < 9 else none for t in (2 * block, 2 * block + 1)], axis=0)
        sums[block * 32:block * 32 + 32, :] = jnp.where(lane < 96, total, pltpu.roll(extra, 96, 1))
    count, depth = sums_ref.shape[0], sums_ref.shape[1]
    for j in range(count):
        sums_ref[j] = sums[j * depth:(j + 1) * depth, :].astype(sums_ref.dtype)


def level_outputs(out_ref, gf_ref, w_fwd, w_gp, fine, act, gpre, keep_gj, flat, turn):
    joiner = iota((256, 128), 0)
    joiner = (2 * ((joiner & 127) - 2) + (joiner >> 7) == iota((256, 128), 1)).astype(F32).astype(BF16)

    def place(values, r):
        values = values.astype(BF16)
        for py in range(2):
            at = (2 * (r - 2) + py) * 32
            flat[at:at + 32, 0:128] = values[py * 64:py * 64 + 32]
            flat[at:at + 32, 128:256] = values[py * 64 + 32:py * 64 + 64]

    def finish(to):
        for part in range(4):
            joined = dot(flat[part * 128:part * 128 + 128, :], joiner)
            for j in range(8):
                turn[pl.ds(part * 8 + j, 16, stride=32), :] = joined[j * 16:j * 16 + 16]
        to[...] = turn[...].astype(BF16)

    for r in range(2, 10):
        got = dot(w_fwd[:, 0:512], fine[(2 * r - 1) * 128:(2 * r + 3) * 128, :])
        got += dot(w_fwd[:, 512:896], act[(r - 2) * 128:(r + 1) * 128, :])
        place(got, r)
    finish(out_ref)
    for r in range(2, 10):
        low = dot(w_gp[...], gpre[(r - 2) * 128:(r + 1) * 128, :]).astype(BF16).astype(F32) * 0.125
        place(keep_gj[(r - 2) * 128:(r - 1) * 128, :] + jnp.concatenate([low] * 8, axis=0), r)
    finish(gf_ref)


def main_kernel(n_wide, n_narrow, f_hbm, c_hbm, fw_hbm, cw_hbm, out_hbm, gf_hbm, total_ref,
                f_ref, c_ref, fw_ref, cw_ref, in_sem,
                wide32, go_left, go_right, ext, left, right, halo_send, halo_recv,
                wide_w, stack, w_fwd, w_bwd, stack_c, w_pre, w_gp,
                fine, cot, pool, act, gpre, keep_gj, flat, turn, sums,
                out_v, gf_v, out_sem, mine, got1, part, got2, fin, send1, recv1, send2, recv2, send3, recv3):
    g1, g2 = n_wide // OUTER, n_narrow * OUTER
    depth = ROWS // g1
    len_y, len_z, len_x = g1 // 2, 2 * OUTER, n_narrow // 2
    me_y, me_x = lax.axis_index("wide"), lax.axis_index("narrow")
    me1 = lax.rem(me_y, g1)
    run_z = lax.div(me_y, g1)
    at_y, at_core = lax.div(me1, 2), lax.rem(me1, 2)
    at_z, at_x = lax.rem(me_x, 2) * OUTER + run_z, lax.div(me_x, 2)
    me2 = at_x * len_z + at_z

    def far_first(sizes):
        steps = [(a, b) for a in range(sizes[0]) for b in range(sizes[1]) if a or b]
        return sorted(steps, key=lambda s: -sum(min(k, n - k) for k, n in zip(s, sizes)))

    first, second = [], []
    for dy, dcore in far_first((len_y, 2)):
        k = lax.rem(at_y + dy, len_y) * 2 + lax.rem(at_core + dcore, 2)
        first.append((k, (run_z * g1 + k, me_x)))
    for dz, dx in far_first((len_z, len_x)):
        z, x = lax.rem(at_z + dz, len_z), lax.rem(at_x + dx, len_x)
        second.append((x * len_z + z, (lax.rem(z, OUTER) * g1 + me1, x * 2 + lax.div(z, OUTER))))

    barrier = pltpu.get_barrier_semaphore()
    near = neighbours(n_wide, n_narrow, me_y, me_x)
    for device in near + [device for _, device in second + first]:
        pl.semaphore_signal(barrier, inc=1, device_id=device, device_id_type=MESH)
    reads = [pltpu.make_async_copy(src, dst, in_sem.at[j]) for j, (src, dst) in enumerate(
        ((f_hbm, f_ref), (c_hbm, c_ref), (fw_hbm, fw_ref), (cw_hbm, cw_ref)))]
    for read in reads:
        read.start()
    for read in reads[:2]:
        read.wait()
    pack_own(f_ref, c_ref, ext, wide32, go_left, go_right)
    pl.semaphore_wait(barrier, 8 + g1 + g2 - 2)
    halo = halo_copies(near, ext, left, right, go_left, go_right, halo_send, halo_recv)
    for j in (4, 5, 6, 7, 2, 3, 0, 1):
        halo[j].start()
    for read in reads[2:]:
        read.wait()
    prepare_weights(fw_ref, cw_ref, wide_w, stack, w_fwd, w_bwd, stack_c, w_pre, w_gp)
    for copy in halo:
        copy.wait_recv()
    level_gradients(n_wide, n_narrow, me_y, me_x, ext, left, right, mine,
                    w_bwd, w_pre, fine, cot, pool, act, gpre, keep_gj, sums)

    def send_all(group, source, slot, sends, receives):
        for j, (k, device) in enumerate(group):
            pltpu.make_async_remote_copy(
                src_ref=source(k), dst_ref=slot(j), send_sem=sends, recv_sem=receives,
                device_id=device, device_id_type=MESH).start()

    def all_of(ref, sends, receives):
        return pltpu.make_async_remote_copy(
            src_ref=ref, dst_ref=ref, send_sem=sends, recv_sem=receives,
            device_id=near[0], device_id_type=MESH)

    one = all_of(got1, send1, recv1)
    two = all_of(got2.at[pl.ds(0, g2 - 1)], send2, recv2)
    three = all_of(fin.at[pl.ds(0, g1 - 1)], send3, recv3)
    send_all(first, lambda k: mine.at[k], lambda j: got1.at[j], send1, recv1)
    level_outputs(out_v, gf_v, w_fwd, w_gp, fine, act, gpre, keep_gj, flat, turn)
    writes = [pltpu.make_async_copy(out_v, out_hbm, out_sem.at[0]), pltpu.make_async_copy(gf_v, gf_hbm, out_sem.at[1])]
    for write in writes:
        write.start()
    one.wait_recv()
    total = mine[me1].astype(F32)
    for j in range(g1 - 1):
        total += got1[j].astype(F32)
    part[...] = total.astype(part.dtype)
    send_all(second, lambda k: part, lambda j: got2.at[me2], send2, recv2)
    got2[me2] = part[...]
    for copy in halo:
        copy.wait_send()
    one.wait_send()
    for write in writes:
        write.wait()
    two.wait_recv()
    total = got2[0].astype(F32)
    for k in range(1, g2):
        total += got2[k].astype(F32)
    fin[me1] = total.astype(fin.dtype)
    send_all(first, lambda k: fin.at[me1], lambda j: fin.at[me1], send3, recv3)
    two.wait_send()
    three.wait_recv()
    for j in range(g1):
        total_ref[j * depth:(j + 1) * depth, :] = fin[j].astype(F32)
    three.wait_send()


def finish_kernel(scale_fine, scale_coarse, turn, out_in, gf_in, gfine_out, gcoarse_out, out_ref, gf_ref,
                  out_v, gf_v, gfine_ref, gcoarse_ref, sem):
    def copy(src, dst, j):
        return pltpu.make_async_copy(src, dst, sem.at[j])

    reads = [copy(out_in, out_v, 1), copy(gf_in, gf_v, 2)]
    writes = [copy(out_v, out_ref, 3), copy(gf_v, gf_ref, 4)]
    for read in reads:
        read.start()
    lane = iota((16, 128), 1)
    for ky in range(3):
        if ky:
            reads[ky - 1].wait()
            writes[ky - 1].start()
        flow = [turn[ky * 32 + z * 16:ky * 32 + z * 16 + 16, :] for z in range(2)]
        rise = [turn[96 + ky * 32 + z * 16:96 + ky * 32 + z * 16 + 16, :] for z in range(2)]
        ups = (rise[1], rise[0] + rise[1], rise[0])
        for kx in range(3):
            near0 = [pltpu.roll(flow[z], (-32 * kx) % 128, 1) if kx else flow[z] for z in range(2)]
            near1 = [pltpu.roll(flow[z], (-32 * kx - 16) % 128, 1) for z in range(2)]
            own = (near0[1], near0[0] + near1[1], near1[0])
            for kz in range(3):
                whole = jnp.where(lane < 16, own[kz], pltpu.roll(ups[kz], (16 - 32 * kx) % 128, 1))
                at = ((ky * 3 + kz) * 3 + kx) * 16
                gfine_ref[at:at + 16, :] = (whole * scale_fine)[:, 0:48]
                if kz == 1:
                    t = ky * 3 + kx
                    row = (t // 2) * 32 + (t % 2) * 16
                    coarse = pltpu.roll(turn[row:row + 16, :], 32, 1)[:, 0:32] * scale_coarse
                    gcoarse_ref[at:at + 16, :] = coarse
                else:
                    gcoarse_ref[at:at + 16, :] = jnp.zeros((16, 32), F32)
        for j, (src, dst) in enumerate(((gfine_ref, gfine_out), (gcoarse_ref, gcoarse_out))):
            rows = pl.ds(ky * 144, 144)
            writes.append(copy(src.at[rows, :], dst.at[rows, :], 5 + 2 * ky + j))
            writes[-1].start()
    for write in writes:
        write.wait()


def shards(n_wide, n_narrow, features, cotangent, coarse_weight, fine_weight):
    inside = pl.BlockSpec(memory_space=VMEM)
    shape = jax.ShapeDtypeStruct
    g1, g2 = n_wide // OUTER, n_narrow * OUTER
    depth = ROWS // g1
    cells = n_wide * 16 * 2 * n_narrow * 128
    fw = jnp.transpose(fine_weight, (2, 3, 4, 0, 1)).reshape(432, 48)
    cw = jnp.transpose(coarse_weight, (2, 3, 4, 1, 0)).reshape(432, 32)
    dma = pltpu.SemaphoreType.DMA
    large = pl.BlockSpec(memory_space=pltpu.HBM)
    output, grad_features, sums = pl.pallas_call(
        functools.partial(main_kernel, n_wide, n_narrow),
        out_shape=(shape((512, 128), BF16), shape((512, 128), BF16), shape((ROWS, 128), F32)),
        in_specs=[large] * 4,
        out_specs=(large, large, inside),
        scratch_shapes=[
            VMEM((512, 128), BF16), VMEM((512, 128), BF16), VMEM((432, 48), BF16), VMEM((432, 32), BF16), dma((4,)),
            VMEM((2, 512, 128), F32), VMEM((16, 512), BF16), VMEM((16, 512), BF16),
            VMEM((2, 768, 128), BF16), VMEM((16, 768), BF16), VMEM((16, 768), BF16), dma((8,)), dma((8,)),
            VMEM((864, 128), F32), VMEM((768, 128), BF16), VMEM((128, 896), BF16), VMEM((160, 512), BF16),
            VMEM((144, 128), BF16), VMEM((32, 144), BF16), VMEM((16, 384), BF16),
            VMEM((3072, 128), BF16), VMEM((3072, 128), BF16), VMEM((576, 128), BF16),
            VMEM((1280, 128), BF16), VMEM((1280, 128), BF16), VMEM((1024, 128), F32),
            VMEM((512, 256), BF16), VMEM((512, 128), F32), VMEM((ROWS, 128), F32),
            VMEM((512, 128), BF16), VMEM((512, 128), BF16), dma((2,)),
            VMEM((g1, depth, 128), F32), VMEM((g1 - 1, depth, 128), F32), VMEM((depth, 128), BF16),
            VMEM((g2, depth, 128), BF16), VMEM((g1, depth, 128), F32),
            dma, dma, dma, dma, dma, dma,
        ],
        compiler_params=pltpu.CompilerParams(
            collective_id=0, has_side_effects=True, vmem_limit_bytes=GRANT),
        name="levels",
    )(features.reshape(512, 128), cotangent.reshape(512, 128), fw, cw)
    gfine, gcoarse, output, grad_features = pl.pallas_call(
        functools.partial(finish_kernel, 1.0 / math.sqrt(cells), 1.0 / math.sqrt(cells // 8)),
        out_shape=(shape((432, 48), F32), shape((432, 32), F32), shape((512, 128), BF16), shape((512, 128), BF16)),
        in_specs=[inside, large, large],
        out_specs=(large,) * 4,
        scratch_shapes=[VMEM((512, 128), BF16), VMEM((512, 128), BF16),
                        VMEM((432, 48), F32), VMEM((432, 32), F32), dma((11,))],
        compiler_params=pltpu.CompilerParams(vmem_limit_bytes=GRANT),
        name="finish",
    )(sums, output, grad_features)
    return (
        output.reshape(16, 16, 2, 128),
        grad_features.reshape(16, 16, 2, 128),
        jnp.transpose(gfine.reshape(3, 3, 3, 16, 48), (3, 4, 0, 1, 2)),
        jnp.transpose(gcoarse.reshape(3, 3, 3, 16, 32), (4, 3, 0, 1, 2)),
    )


def solution(mesh):
    placed = P(None, "wide", None, "narrow")
    return jax.shard_map(
        functools.partial(shards, mesh.shape["wide"], mesh.shape["narrow"]),
        mesh=mesh,
        in_specs=(placed, placed, P(), P()),
        out_specs=(placed, placed, P(), P()),
        check_vma=False,
    )
```
